32 devices in a mesh: grp: 2 (over y), beam: 8 (over z, x), gy: 2 (over core).
Axes of the slice: x: 2, y: 2, z: 4, core: 2. Of those that a mesh axis runs over, the one named last changes fastest.
Arguments:
- concentration: float32 [16, 32, 16, 256], P('grp', 'beam', None, 'gy'), parts along dimension 0, may hold values from 0.2 to 2
- incident_mu: float32 [8], replicated, may hold values from 0.003125 to 0.03125
- exit_mu: float32 [3, 8], replicated, may hold values from 0.000390625 to 0.00390625
- line_element: int32 [3], replicated, may hold values from 0 to 7
- tilt_index: int32 [1], replicated, may hold values from 0 to 63
- shear: int32 [32], P('grp'), parts along dimension 0, may hold values from 0 to 15
- data: float32 [128, 3, 16, 256], P('grp', None, None, 'gy'), parts along dimension 0, may hold values from 1.6 to 16
Outputs:
- updated: float32 [16, 32, 16, 256], P('grp', 'beam', None, 'gy'), parts along dimension 0
The draws below stay inside these ranges and needn't reach their ends.
There are 2 independent parts, one for each index of `grp`. The reference program is written for one: setup_inputs(seed, part) draws one part's arguments, and reference() takes and returns one part's arrays. A program takes and returns all parts, laid end to end along the dimension named above; an argument that names none is the same for every part. Nothing has to cross between parts.
All inputs are finite; a program needn't handle non-finite values.
Results may differ from the reference program's by a relative error of at most 0.000067.
Values sent between devices are 32-bit elements; how exact they have to be, the bound alone decides.
A program may use at most 64 MiB of HBM per device.

```python
import math
import jax
import jax.numpy as jnp
from jax import lax

E = 8
L = 3
NZ = 16
TILTS = 64
NB = 32
NY = 256


def set_ends(array, key, least, high):
    shape = array.shape
    spot = [jax.random.randint(jax.random.fold_in(key, axis), (), 0, shape[axis]) for axis in range(len(shape))]
    array = array.at[tuple(spot)].set(least)
    longest = shape.index(max(shape))
    spot[longest] = (spot[longest] + 1) % shape[longest]
    return array.at[tuple(spot)].set(high)


def shard_levels(key, extent, split, low, high):
    factor_of = 1.0
    for dim, shards_of in split:
        draws = jax.random.uniform(jax.random.fold_in(jax.random.fold_in(key, 6), dim), (shards_of,), jnp.float32, low / len(split), high / len(split))
        factor_of = factor_of * jnp.repeat(jnp.exp(draws), extent[dim] // shards_of).reshape((-1,) + (1,) * (len(extent) - 1 - dim))
    return factor_of


def setup_inputs(seed: int = 0, part: int = 0) -> dict:
    arg_keys = jax.random.split(jax.random.key(seed), 8)
    part_keys = jax.random.split(jax.random.fold_in(arg_keys[7], part), 8)
    concentration = jnp.clip(jnp.exp(math.log(2.0) - 2.3025851 * jax.random.uniform(part_keys[0], (E, NB, NZ, NY), jnp.float32) ** shard_levels(part_keys[0], (E, NB, NZ, NY), ((1, 8), (3, 2)), -0.2, 0.2)), 0.2, 2.0)
    incident_mu = jnp.clip(jnp.exp(jax.random.uniform(arg_keys[1], (E,), jnp.float32, math.log(0.003125), math.log(0.03125))), 0.003125, 0.03125)
    exit_mu = jnp.clip(jnp.exp(jax.random.uniform(arg_keys[2], (L, E), jnp.float32, math.log(0.000390625), math.log(0.00390625))), 0.000390625, 0.00390625)
    line_element = jax.random.randint(arg_keys[3], (L,), 0, E).astype(jnp.int32)
    tilt_index = jax.random.randint(arg_keys[4], (1,), 0, TILTS).astype(jnp.int32)
    shear = set_ends(jax.random.randint(part_keys[5], (NZ,), 0, NB // 2), jax.random.fold_in(part_keys[5], 1), 0, (NB // 2) - 1).astype(jnp.int32)
    data = jnp.clip(jnp.exp(math.log(16.0) - 2.3025851 * jax.random.uniform(part_keys[6], (TILTS, L, NZ, NY), jnp.float32) ** shard_levels(part_keys[6], (TILTS, L, NZ, NY), ((3, 2),), -0.2, 0.2)), 1.6, 16.0)
    return {"concentration": concentration, "incident_mu": incident_mu, "exit_mu": exit_mu, "line_element": line_element, "tilt_index": tilt_index, "shear": shear, "data": data}


blend_weight = 0.05


def reference(concentration, incident_mu, exit_mu, line_element, tilt_index, shear, data):
    beam_cells = jnp.arange(NB, dtype=jnp.int32)
    support = (beam_cells[:, None] >= shear[None, :]).astype(jnp.float32)
    live_cells = concentration * support[None, :, :, None]
    incident_rate = jnp.einsum("e,ebzy->bzy", incident_mu, live_cells, precision=lax.Precision.HIGHEST)
    depth_in = jnp.cumsum(incident_rate, axis=0) - 0.5 * incident_rate
    incident = jnp.exp(-depth_in)
    exit_rate = jnp.einsum("le,ebzy->lbzy", exit_mu, live_cells, precision=lax.Precision.HIGHEST)
    exit_path = jnp.flip(jnp.cumsum(jnp.flip(exit_rate, 3), axis=3), 3) - 0.5 * exit_rate
    weight = incident[None] * jnp.exp(-exit_path)
    onehot = (line_element[:, None] == jnp.arange(E, dtype=jnp.int32)[None, :]).astype(jnp.float32)
    source = jnp.einsum("le,ebzy->lbzy", onehot, live_cells, precision=lax.Precision.HIGHEST)
    emission = jnp.sum(weight * source, axis=1)
    measured = lax.dynamic_index_in_dim(data, tilt_index[0], 0, keepdims=False)
    ratios = measured / emission
    kept_weight = weight * support[None, :, :, None]
    numerator = blend_weight + jnp.einsum("le,lbzy->ebzy", onehot, kept_weight * ratios[:, None], precision=lax.Precision.HIGHEST)
    denominator = blend_weight + jnp.einsum("le,lbzy->ebzy", onehot, kept_weight, precision=lax.Precision.HIGHEST)
    return concentration * numerator / denominator
```

```python
import functools

import jax
import jax.numpy as jnp
from jax import lax
from jax.experimental import pallas as pl
from jax.experimental.pallas import tpu as pltpu
from jax.sharding import PartitionSpec as P

blend_weight = 0.05
MESH = pl.DeviceIdType.MESH


def loop(count, body):
    if count <= 16:
        for step in range(count):
            body(step)
    else:

        def one(step, carry):
            body(step)
            return carry

        lax.fori_loop(0, count, one, 0)


def fold(count, body, carry):
    if count <= 16:
        for step in range(count):
            carry = body(step, carry)
        return carry
    return lax.fori_loop(0, count, body, carry)


def layout(slices, bricks, lines):
    owners = min(slices, bricks)
    while slices % owners or bricks % owners:
        owners -= 1
    chunk = slices // owners
    rows = -(-(lines + 1) * chunk // 8) * 8
    return owners, bricks // owners, chunk, rows


def kernel(
    bricks,
    slabs,
    conc_hbm,
    incident_hbm,
    exit_hbm,
    line_hbm,
    tilt_hbm,
    shear_hbm,
    data_hbm,
    factor,
    conc,
    data,
    incident_mu,
    exit_mu,
    line,
    tilt,
    shear,
    weight,
    slab_out,
    slab_in,
    sent,
    taken,
    reply,
    back,
    measured,
    load_sem,
    slab_send,
    slab_recv,
    out_send,
    out_recv,
    back_send,
    back_recv,
):
    elements, cells, slices, width = conc.shape
    lines = exit_mu.shape[0]
    owners, stride, chunk, rows = layout(slices, bricks, lines)
    me = lax.axis_index("beam")
    slab = lax.axis_index("gy")
    rank = me if stride == 1 else me // stride
    is_owner = True if stride == 1 else lax.rem(me, stride) == 0

    loads = [
        pltpu.make_async_copy(src, dst, load_sem.at[k])
        for k, (src, dst) in enumerate(
            (
                (conc_hbm, conc),
                (exit_hbm, exit_mu),
                (shear_hbm, shear),
                (incident_hbm, incident_mu),
                (line_hbm, line),
                (tilt_hbm, tilt),
                (data_hbm, data),
            )
        )
    ]
    for load in loads:
        load.start()

    def when(condition, body):
        if condition is True:
            body()
        else:
            pl.when(condition)(body)

    def other_bricks(body):
        if bricks <= 16:
            for k in range(1, bricks):
                body(lax.rem(me + k, bricks))
        else:
            loop(bricks, lambda s: pl.when(s != me)(lambda: body(s)))

    def other_owners(body):
        if stride == 1:
            other_bricks(lambda s: body(s, s))
        else:
            loop(owners, lambda j: pl.when(j * stride != me)(lambda: body(j, j * stride)))

    barrier = pltpu.get_barrier_semaphore()

    def greet_brick(s):
        pl.semaphore_signal(barrier, inc=1, device_id={"beam": s}, device_id_type=MESH)

    def greet_owner(j, s):
        greet_brick(s)

    for d in range(1, slabs):
        pl.semaphore_signal(
            barrier,
            inc=1,
            device_id={"gy": lax.rem(slab + d, slabs)},
            device_id_type=MESH,
        )
    if stride == 1:
        other_bricks(greet_brick)
    else:
        pl.when(is_owner)(lambda: other_bricks(greet_brick))
        pl.when(jnp.logical_not(is_owner))(lambda: other_owners(greet_owner))

    def side(shape, axis):
        return lax.broadcasted_iota(jnp.int32, shape, axis)

    square = (2 * width, 2 * width)
    row = lax.rem(side(square, 0), width)
    column = side(square, 1)
    sums = jnp.where(
        column >= width, 1.0, jnp.where(row > column, 1.0, jnp.where(row == column, 0.5, 0.0))
    ).astype(jnp.bfloat16)

    tile = (slices, width)
    z_of = side(tile, 0)
    lane = side(tile, 1)
    for load in loads[:-1]:
        load.wait()
    first = jnp.zeros(tile, jnp.int32)
    for z in range(slices):
        first = jnp.where(z_of == z, shear[z], first)
    support = [
        jnp.where(me * cells + b >= first, 1.0, 0.0).astype(jnp.float32) for b in range(cells)
    ]
    exit_rate = []
    for l in range(lines):
        for b in range(cells):
            total = conc[0, b] * exit_mu[l, 0]
            for e in range(1, elements):
                total += conc[e, b] * exit_mu[l, e]
            exit_rate.append(total * support[b])
    stacked = jnp.concatenate(exit_rate, axis=0)
    high = stacked.astype(jnp.bfloat16)
    low = (stacked - high.astype(jnp.float32)).astype(jnp.bfloat16)
    paths = jnp.dot(
        jnp.concatenate([high, low], axis=1), sums, preferred_element_type=jnp.float32
    )

    packed = jnp.zeros(tile, jnp.float32)
    for c in range(lines * cells):
        packed = jnp.where(lane == c, paths[c * slices : (c + 1) * slices, width:], packed)
    slab_out[...] = packed

    def slab_copy(d, target):
        return pltpu.make_async_remote_copy(
            src_ref=slab_out,
            dst_ref=slab_in.at[d - 1],
            send_sem=slab_send.at[d - 1],
            recv_sem=slab_recv.at[d - 1],
            device_id={"gy": target},
            device_id_type=MESH,
        )

    if stride == 1:
        pl.semaphore_wait(barrier, bricks - 1 + slabs - 1)
    else:
        pl.when(is_owner)(lambda: pl.semaphore_wait(barrier, bricks - 1 + slabs - 1))
        pl.when(jnp.logical_not(is_owner))(
            lambda: pl.semaphore_wait(barrier, owners + slabs - 1)
        )
    for d in range(1, slabs):
        pl.when(slab >= d)(lambda d=d: slab_copy(d, slab - d).start())

    before = jnp.zeros(tile, jnp.float32)
    for b in range(cells):
        rate = conc[0, b] * incident_mu[0]
        for e in range(1, elements):
            rate += conc[e, b] * incident_mu[e]
        rate *= support[b]
        depth = before + 0.5 * rate
        before += rate
        for l in range(lines):
            c = l * cells + b
            path = paths[c * slices : (c + 1) * slices, :width]
            weight[c] = support[b] * jnp.exp(-(depth + path))

    def put(q, value):
        for i in range(chunk):
            sent[pl.ds(q * chunk + i, owners, stride=rows), :] = value[
                i * owners : (i + 1) * owners
            ]

    put(0, before)
    if rows > (lines + 1) * chunk:
        for r in range((lines + 1) * chunk, rows):
            sent[pl.ds(r, owners, stride=rows), :] = jnp.zeros((owners, width), jnp.float32)

    for d in range(1, slabs):

        @pl.when(slab + d < slabs)
        def _(d=d):
            slab_copy(d, slab - d).wait_recv()
            passed = jnp.exp(-slab_in[d - 1])
            for c in range(lines * cells):
                weight[c] *= jnp.broadcast_to(passed[:, c : c + 1], tile)

    for l in range(lines):
        source = line[l]
        partial = weight[l * cells] * conc[source, 0]
        for b in range(1, cells):
            partial += weight[l * cells + b] * conc[source, b]
        put(l + 1, partial)

    def part(j):
        return pl.ds(pl.multiple_of(j * rows, 8), rows)

    def out_copy(j, target, source):
        return pltpu.make_async_remote_copy(
            src_ref=sent.at[part(j)],
            dst_ref=taken.at[source],
            send_sem=out_send.at[j],
            recv_sem=out_recv.at[source],
            device_id={"beam": target},
            device_id_type=MESH,
        )

    def back_copy(j, target):
        return pltpu.make_async_remote_copy(
            src_ref=reply.at[target],
            dst_ref=back.at[part(j)],
            send_sem=back_send.at[target],
            recv_sem=back_recv.at[j],
            device_id={"beam": target},
            device_id_type=MESH,
        )

    other_owners(lambda j, s: out_copy(j, s, me).start())

    loads[-1].wait()
    for j in range(1):
        for l in range(lines):
            values = data[tilt[0], l]
            for i in range(chunk):
                measured[pl.ds((l + 1) * chunk + i, owners, stride=rows), :] = values[
                    i * owners : (i + 1) * owners
                ]
    for r in list(range(chunk)) + list(range((lines + 1) * chunk, rows)):
        measured[pl.ds(r, owners, stride=rows), :] = jnp.zeros((owners, width), jnp.float32)

    def own():
        taken[me] = sent[part(rank), :]
        other_bricks(lambda s: out_copy(rank, s, s).wait_recv())
        head = side((rows, width), 0) < chunk

        def one(s, carry):
            run, emission = carry
            start = jnp.where(head, run, 0.0)
            spread = start
            for q in range(1, lines + 1):
                spread += pltpu.roll(start, q * chunk, 0)
            passed = jnp.exp(-spread)
            reply[s] = passed
            values = taken[s]
            return run + values, emission + passed * values

        zero = jnp.zeros((rows, width), jnp.float32)
        _, emission = fold(bricks, one, (zero, zero))
        ratio = measured[part(rank), :] / emission

        def finish(s):
            reply[s] = jnp.where(head, reply[s], ratio)

        loop(bricks, finish)
        other_bricks(lambda s: back_copy(rank, s).start())
        back[part(rank), :] = reply[me]

    when(is_owner, own)
    other_owners(lambda j, s: back_copy(j, me).wait_recv())

    def get(q):
        return jnp.concatenate(
            [back[pl.ds(q * chunk + i, owners, stride=rows), :] for i in range(chunk)], axis=0
        )

    arrived = get(0)
    ratios = [get(l + 1) for l in range(lines)]
    same = [
        [jnp.where(line[l] == line[k], 1.0, 0.0).astype(jnp.float32) for k in range(lines)]
        for l in range(lines)
    ]
    for b in range(cells):
        kept = [weight[l * cells + b] * arrived for l in range(lines)]
        raised = [kept[l] * ratios[l] for l in range(lines)]
        for l in range(lines):
            top = blend_weight + raised[l]
            bottom = blend_weight + kept[l]
            for k in range(lines):
                if k != l:
                    top += same[l][k] * raised[k]
                    bottom += same[l][k] * kept[k]
            factor[l, b] = top / bottom

    other_owners(lambda j, s: out_copy(j, s, me).wait_send())
    when(is_owner, lambda: other_bricks(lambda s: back_copy(rank, s).wait_send()))
    for d in range(1, slabs):
        pl.when(slab >= d)(lambda d=d: slab_copy(d, slab - d).wait_send())


def per_device(
    bricks, slabs, concentration, incident_mu, exit_mu, line_element, tilt_index, shear, data
):
    elements, cells, slices, width = concentration.shape
    lines = exit_mu.shape[0]
    owners, _, _, rows = layout(slices, bricks, lines)
    f32 = jnp.float32
    factor = pl.pallas_call(
        functools.partial(kernel, bricks, slabs),
        out_shape=jax.ShapeDtypeStruct((lines, cells, slices, width), f32),
        in_specs=[pl.BlockSpec(memory_space=pl.ANY)] * 7,
        out_specs=pl.BlockSpec(memory_space=pltpu.VMEM),
        scratch_shapes=[
            pltpu.VMEM(concentration.shape, f32),
            pltpu.VMEM(data.shape, f32),
            pltpu.SMEM(incident_mu.shape, f32),
            pltpu.SMEM(exit_mu.shape, f32),
            pltpu.SMEM(line_element.shape, jnp.int32),
            pltpu.SMEM(tilt_index.shape, jnp.int32),
            pltpu.SMEM(shear.shape, jnp.int32),
            pltpu.VMEM((lines * cells, slices, width), f32),
            pltpu.VMEM((slices, width), f32),
            pltpu.VMEM((max(slabs - 1, 1), slices, width), f32),
            pltpu.VMEM((owners * rows, width), f32),
            pltpu.VMEM((bricks, rows, width), f32),
            pltpu.VMEM((bricks, rows, width), f32),
            pltpu.VMEM((owners * rows, width), f32),
            pltpu.VMEM((owners * rows, width), f32),
            pltpu.SemaphoreType.DMA((7,)),
            pltpu.SemaphoreType.DMA((max(slabs - 1, 1),)),
            pltpu.SemaphoreType.DMA((max(slabs - 1, 1),)),
            pltpu.SemaphoreType.DMA((owners,)),
            pltpu.SemaphoreType.DMA((bricks,)),
            pltpu.SemaphoreType.DMA((bricks,)),
            pltpu.SemaphoreType.DMA((owners,)),
        ],
        compiler_params=pltpu.CompilerParams(
            collective_id=0, has_side_effects=True, vmem_limit_bytes=16 * 1024 * 1024
        ),
        name="update_factor",
    )(concentration, incident_mu, exit_mu, line_element, tilt_index, shear, data)
    element = lax.broadcasted_iota(jnp.int32, concentration.shape, 0)
    scale = jnp.ones_like(concentration)
    for l in range(lines):
        scale = jnp.where(element == line_element[l], factor[l][None], scale)
    return concentration * scale


def solution(mesh):
    placed = (
        P("grp", "beam", None, "gy"),
        P(),
        P(),
        P(),
        P(),
        P("grp"),
        P("grp", None, None, "gy"),
    )
    return jax.shard_map(
        functools.partial(per_device, mesh.shape["beam"], mesh.shape["gy"]),
        mesh=mesh,
        in_specs=placed,
        out_specs=P("grp", "beam", None, "gy"),
        check_vma=False,
    )
```

```python
import functools

import jax
import jax.numpy as jnp
from jax import lax
from jax.experimental import pallas as pl
from jax.experimental.pallas import tpu as pltpu
from jax.sharding import PartitionSpec as P

blend_weight = 0.05
MESH = pl.DeviceIdType.MESH


def loop(count, body):
    if count <= 16:
        for step in range(count):
            body(step)
    else:

        def one(step, carry):
            body(step)
            return carry

        lax.fori_loop(0, count, one, 0)


def fold(count, body, carry):
    if count <= 16:
        for step in range(count):
            carry = body(step, carry)
        return carry
    return lax.fori_loop(0, count, body, carry)


def layout(slices, bricks, lines):
    owners = min(slices, bricks)
    while slices % owners or bricks % owners:
        owners -= 1
    chunk = slices // owners
    rows = -(-(lines + 1) * chunk // 8) * 8
    return owners, bricks // owners, chunk, rows


def kernel(
    bricks,
    slabs,
    conc_hbm,
    incident_hbm,
    exit_hbm,
    line_hbm,
    tilt_hbm,
    shear_hbm,
    data_hbm,
    updated,
    conc,
    data,
    incident_mu,
    exit_mu,
    line,
    tilt,
    shear,
    weight,
    slab_out,
    slab_in,
    sent,
    taken,
    reply,
    back,
    measured,
    load_sem,
    slab_send,
    slab_recv,
    out_send,
    out_recv,
    back_send,
    back_recv,
):
    elements, cells, slices, width = conc.shape
    lines = exit_mu.shape[0]
    owners, stride, chunk, rows = layout(slices, bricks, lines)
    me = lax.axis_index("beam")
    slab = lax.axis_index("gy")
    rank = me if stride == 1 else me // stride
    is_owner = True if stride == 1 else lax.rem(me, stride) == 0

    loads = [
        pltpu.make_async_copy(src, dst, load_sem.at[k])
        for k, (src, dst) in enumerate(
            (
                (conc_hbm, conc),
                (exit_hbm, exit_mu),
                (shear_hbm, shear),
                (incident_hbm, incident_mu),
                (line_hbm, line),
                (tilt_hbm, tilt),
                (data_hbm, data),
            )
        )
    ]
    for load in loads:
        load.start()

    def when(condition, body):
        if condition is True:
            body()
        else:
            pl.when(condition)(body)

    def other_bricks(body):
        if bricks <= 16:
            for k in range(1, bricks):
                body(lax.rem(me + k, bricks))
        else:
            loop(bricks, lambda s: pl.when(s != me)(lambda: body(s)))

    def other_owners(body):
        if stride == 1:
            other_bricks(lambda s: body(s, s))
        else:
            loop(owners, lambda j: pl.when(j * stride != me)(lambda: body(j, j * stride)))

    barrier = pltpu.get_barrier_semaphore()

    def greet_brick(s):
        pl.semaphore_signal(barrier, inc=1, device_id={"beam": s}, device_id_type=MESH)

    def greet_owner(j, s):
        greet_brick(s)

    for d in range(1, slabs):
        pl.semaphore_signal(
            barrier,
            inc=1,
            device_id={"gy": lax.rem(slab + d, slabs)},
            device_id_type=MESH,
        )
    if stride == 1:
        other_bricks(greet_brick)
    else:
        pl.when(is_owner)(lambda: other_bricks(greet_brick))
        pl.when(jnp.logical_not(is_owner))(lambda: other_owners(greet_owner))

    def side(shape, axis):
        return lax.broadcasted_iota(jnp.int32, shape, axis)

    square = (2 * width, 2 * width)
    row = lax.rem(side(square, 0), width)
    column = side(square, 1)
    sums = jnp.where(
        column >= width, 1.0, jnp.where(row > column, 1.0, jnp.where(row == column, 0.5, 0.0))
    ).astype(jnp.bfloat16)

    tile = (slices, width)
    z_of = side(tile, 0)
    lane = side(tile, 1)
    for load in loads[:-1]:
        load.wait()
    first = jnp.zeros(tile, jnp.int32)
    for z in range(slices):
        first = jnp.where(z_of == z, shear[z], first)
    support = [
        jnp.where(me * cells + b >= first, 1.0, 0.0).astype(jnp.float32) for b in range(cells)
    ]
    exit_rate = []
    for l in range(lines):
        for b in range(cells):
            total = conc[0, b] * exit_mu[l, 0]
            for e in range(1, elements):
                total += conc[e, b] * exit_mu[l, e]
            exit_rate.append(total * support[b])
    stacked = jnp.concatenate(exit_rate, axis=0)
    high = stacked.astype(jnp.bfloat16)
    low = (stacked - high.astype(jnp.float32)).astype(jnp.bfloat16)
    paths = jnp.dot(
        jnp.concatenate([high, low], axis=1), sums, preferred_element_type=jnp.float32
    )

    packed = jnp.zeros(tile, jnp.float32)
    for c in range(lines * cells):
        packed = jnp.where(lane == c, paths[c * slices : (c + 1) * slices, width:], packed)
    slab_out[...] = packed

    def slab_copy(d, target):
        return pltpu.make_async_remote_copy(
            src_ref=slab_out,
            dst_ref=slab_in.at[d - 1],
            send_sem=slab_send.at[d - 1],
            recv_sem=slab_recv.at[d - 1],
            device_id={"gy": target},
            device_id_type=MESH,
        )

    if stride == 1:
        pl.semaphore_wait(barrier, bricks - 1 + slabs - 1)
    else:
        pl.when(is_owner)(lambda: pl.semaphore_wait(barrier, bricks - 1 + slabs - 1))
        pl.when(jnp.logical_not(is_owner))(
            lambda: pl.semaphore_wait(barrier, owners + slabs - 1)
        )
    for d in range(1, slabs):
        pl.when(slab >= d)(lambda d=d: slab_copy(d, slab - d).start())

    before = jnp.zeros(tile, jnp.float32)
    for b in range(cells):
        rate = conc[0, b] * incident_mu[0]
        for e in range(1, elements):
            rate += conc[e, b] * incident_mu[e]
        rate *= support[b]
        depth = before + 0.5 * rate
        before += rate
        for l in range(lines):
            c = l * cells + b
            path = paths[c * slices : (c + 1) * slices, :width]
            weight[c] = support[b] * jnp.exp(-(depth + path))

    def put(q, value):
        for i in range(chunk):
            sent[pl.ds(q * chunk + i, owners, stride=rows), :] = value[
                i * owners : (i + 1) * owners
            ]

    put(0, before)
    if rows > (lines + 1) * chunk:
        for r in range((lines + 1) * chunk, rows):
            sent[pl.ds(r, owners, stride=rows), :] = jnp.zeros((owners, width), jnp.float32)

    for d in range(1, slabs):

        @pl.when(slab + d < slabs)
        def _(d=d):
            slab_copy(d, slab - d).wait_recv()
            passed = jnp.exp(-slab_in[d - 1])
            for c in range(lines * cells):
                weight[c] *= jnp.broadcast_to(passed[:, c : c + 1], tile)

    for l in range(lines):
        source = line[l]
        partial = weight[l * cells] * conc[source, 0]
        for b in range(1, cells):
            partial += weight[l * cells + b] * conc[source, b]
        put(l + 1, partial)

    def part(j):
        return pl.ds(pl.multiple_of(j * rows, 8), rows)

    def out_copy(j, target, source):
        return pltpu.make_async_remote_copy(
            src_ref=sent.at[part(j)],
            dst_ref=taken.at[source],
            send_sem=out_send.at[j],
            recv_sem=out_recv.at[source],
            device_id={"beam": target},
            device_id_type=MESH,
        )

    def back_copy(j, target):
        return pltpu.make_async_remote_copy(
            src_ref=reply.at[target],
            dst_ref=back.at[part(j)],
            send_sem=back_send.at[target],
            recv_sem=back_recv.at[j],
            device_id={"beam": target},
            device_id_type=MESH,
        )

    other_owners(lambda j, s: out_copy(j, s, me).start())

    loads[-1].wait()
    for l in range(lines):
        values = data[tilt[0], l]
        for i in range(chunk):
            measured[pl.ds((l + 1) * chunk + i, owners, stride=rows), :] = values[
                i * owners : (i + 1) * owners
            ]
    for r in list(range(chunk)) + list(range((lines + 1) * chunk, rows)):
        measured[pl.ds(r, owners, stride=rows), :] = jnp.zeros((owners, width), jnp.float32)

    def own():
        taken[me] = sent[part(rank), :]
        other_bricks(lambda s: out_copy(rank, s, s).wait_recv())
        head = side((rows, width), 0) < chunk

        def one(s, carry):
            run, emission = carry
            start = jnp.where(head, run, 0.0)
            spread = start
            for q in range(1, lines + 1):
                spread += pltpu.roll(start, q * chunk, 0)
            passed = jnp.exp(-spread)
            reply[s] = passed
            values = taken[s]
            return run + values, emission + passed * values

        zero = jnp.zeros((rows, width), jnp.float32)
        _, emission = fold(bricks, one, (zero, zero))
        ratio = measured[part(rank), :] / emission

        def finish(s):
            reply[s] = jnp.where(head, reply[s], ratio)

        loop(bricks, finish)
        other_bricks(lambda s: back_copy(rank, s).start())
        back[part(rank), :] = reply[me]

    when(is_owner, own)
    other_owners(lambda j, s: back_copy(j, me).wait_recv())

    def get(q):
        return jnp.concatenate(
            [back[pl.ds(q * chunk + i, owners, stride=rows), :] for i in range(chunk)], axis=0
        )

    arrived = get(0)
    ratios = [get(l + 1) for l in range(lines)]
    same = [
        [jnp.where(line[l] == line[k], 1.0, 0.0).astype(jnp.float32) for k in range(lines)]
        for l in range(lines)
    ]
    for b in range(cells):
        kept = [weight[l * cells + b] * arrived for l in range(lines)]
        raised = [kept[l] * ratios[l] for l in range(lines)]
        factor = []
        for l in range(lines):
            top = blend_weight + raised[l]
            bottom = blend_weight + kept[l]
            for k in range(lines):
                if k != l:
                    top += same[l][k] * raised[k]
                    bottom += same[l][k] * kept[k]
            factor.append(top / bottom)
        for e in range(elements):
            scale = 1.0
            for l in range(lines):
                scale = jnp.where(line[l] == e, factor[l], scale)
            updated[e, b] = conc[e, b] * scale

    other_owners(lambda j, s: out_copy(j, s, me).wait_send())
    when(is_owner, lambda: other_bricks(lambda s: back_copy(rank, s).wait_send()))
    for d in range(1, slabs):
        pl.when(slab >= d)(lambda d=d: slab_copy(d, slab - d).wait_send())


def per_device(
    bricks, slabs, concentration, incident_mu, exit_mu, line_element, tilt_index, shear, data
):
    elements, cells, slices, width = concentration.shape
    lines = exit_mu.shape[0]
    owners, _, _, rows = layout(slices, bricks, lines)
    f32 = jnp.float32
    arguments = (concentration, incident_mu, exit_mu, line_element, tilt_index, shear, data)
    return pl.pallas_call(
        functools.partial(kernel, bricks, slabs),
        out_shape=pltpu.VMEM(concentration.shape, f32),
        in_specs=[pl.BlockSpec(memory_space=pl.ANY)] * 7,
        out_specs=pl.BlockSpec(memory_space=pltpu.VMEM),
        scratch_shapes=[
            pltpu.VMEM(concentration.shape, f32),
            pltpu.VMEM(data.shape, f32),
            pltpu.SMEM(incident_mu.shape, f32),
            pltpu.SMEM(exit_mu.shape, f32),
            pltpu.SMEM(line_element.shape, jnp.int32),
            pltpu.SMEM(tilt_index.shape, jnp.int32),
            pltpu.SMEM(shear.shape, jnp.int32),
            pltpu.VMEM((lines * cells, slices, width), f32),
            pltpu.VMEM((slices, width), f32),
            pltpu.VMEM((max(slabs - 1, 1), slices, width), f32),
            pltpu.VMEM((owners * rows, width), f32),
            pltpu.VMEM((bricks, rows, width), f32),
            pltpu.VMEM((bricks, rows, width), f32),
            pltpu.VMEM((owners * rows, width), f32),
            pltpu.VMEM((owners * rows, width), f32),
            pltpu.SemaphoreType.DMA((7,)),
            pltpu.SemaphoreType.DMA((max(slabs - 1, 1),)),
            pltpu.SemaphoreType.DMA((max(slabs - 1, 1),)),
            pltpu.SemaphoreType.DMA((owners,)),
            pltpu.SemaphoreType.DMA((bricks,)),
            pltpu.SemaphoreType.DMA((bricks,)),
            pltpu.SemaphoreType.DMA((owners,)),
        ],
        compiler_params=pltpu.CompilerParams(
            collective_id=0, has_side_effects=True, vmem_limit_bytes=16 * 1024 * 1024
        ),
        name="update",
    )(*(x if x.size == 1 else pltpu.with_memory_space_constraint(x, pltpu.HBM) for x in arguments))


def solution(mesh):
    placed = (
        P("grp", "beam", None, "gy"),
        P(),
        P(),
        P(),
        P(),
        P("grp"),
        P("grp", None, None, "gy"),
    )
    return jax.shard_map(
        functools.partial(per_device, mesh.shape["beam"], mesh.shape["gy"]),
        mesh=mesh,
        in_specs=placed,
        out_specs=P("grp", "beam", None, "gy"),
        check_vma=False,
    )
```

```python
import functools

import jax
import jax.numpy as jnp
from jax import lax
from jax.experimental import pallas as pl
from jax.experimental.pallas import tpu as pltpu
from jax.sharding import PartitionSpec as P

blend_weight = 0.05
MESH = pl.DeviceIdType.MESH


def loop(count, body):
    if count <= 16:
        for step in range(count):
            body(step)
    else:

        def one(step, carry):
            body(step)
            return carry

        lax.fori_loop(0, count, one, 0)


def fold(count, body, carry):
    if count <= 16:
        for step in range(count):
            carry = body(step, carry)
        return carry
    return lax.fori_loop(0, count, body, carry)


def layout(slices, bricks, lines):
    owners = min(slices, bricks)
    while slices % owners or bricks % owners:
        owners -= 1
    chunk = slices // owners
    rows = -(-(lines + 1) * chunk // 8) * 8
    return owners, bricks // owners, chunk, rows


def kernel(
    bricks,
    slabs,
    conc_hbm,
    incident_hbm,
    exit_hbm,
    line_hbm,
    tilt_hbm,
    shear_hbm,
    data_hbm,
    updated,
    conc,
    data,
    incident_mu,
    exit_mu,
    line,
    tilt,
    shear,
    weight,
    slab_out,
    slab_in,
    near_out,
    near_in,
    sent,
    taken,
    reply,
    back,
    measured,
    load_sem,
    slab_send,
    slab_recv,
    near_send,
    near_recv,
    out_send,
    out_recv,
    back_send,
    back_recv,
):
    elements, cells, slices, width = conc.shape
    lines = exit_mu.shape[0]
    owners, stride, chunk, rows = layout(slices, bricks, lines)
    me = lax.axis_index("beam")
    slab = lax.axis_index("gy")
    rank = me if stride == 1 else me // stride
    is_owner = True if stride == 1 else lax.rem(me, stride) == 0

    loads = [
        pltpu.make_async_copy(src, dst, load_sem.at[k])
        for k, (src, dst) in enumerate(
            (
                (conc_hbm, conc),
                (exit_hbm, exit_mu),
                (shear_hbm, shear),
                (incident_hbm, incident_mu),
                (line_hbm, line),
                (tilt_hbm, tilt),
                (data_hbm, data),
            )
        )
    ]
    for load in loads:
        load.start()

    def when(condition, body):
        if condition is True:
            body()
        else:
            pl.when(condition)(body)

    def other_bricks(body):
        if bricks <= 16:
            for k in range(1, bricks):
                body(lax.rem(me + k, bricks))
        else:
            loop(bricks, lambda s: pl.when(s != me)(lambda: body(s)))

    def other_owners(body):
        if stride == 1:
            other_bricks(lambda s: body(s, s))
        else:
            loop(owners, lambda j: pl.when(j * stride != me)(lambda: body(j, j * stride)))

    barrier = pltpu.get_barrier_semaphore()

    def greet_brick(s):
        pl.semaphore_signal(barrier, inc=1, device_id={"beam": s}, device_id_type=MESH)

    def greet_owner(j, s):
        greet_brick(s)

    def greet_later(brick):
        for d in range(1, slabs):

            @pl.when(slab + d < slabs)
            def _(d=d):
                pl.semaphore_signal(
                    barrier,
                    inc=1,
                    device_id={"beam": brick, "gy": slab + d},
                    device_id_type=MESH,
                )

    def greet_as_owner():
        other_bricks(greet_brick)
        loop(bricks, greet_later)

    def greet_as_other():
        other_owners(greet_owner)
        greet_later(me)

    when(is_owner, greet_as_owner)
    if stride > 1:
        pl.when(jnp.logical_not(is_owner))(greet_as_other)

    def wait_barrier():
        when(is_owner, lambda: pl.semaphore_wait(barrier, bricks - 1 + slab * owners))
        if stride > 1:
            pl.when(jnp.logical_not(is_owner))(
                lambda: pl.semaphore_wait(barrier, owners + slab * (owners + 1))
            )

    def side(shape, axis):
        return lax.broadcasted_iota(jnp.int32, shape, axis)

    square = (2 * width, 2 * width)
    row = lax.rem(side(square, 0), width)
    column = side(square, 1)
    sums = jnp.where(
        column >= width, 1.0, jnp.where(row > column, 1.0, jnp.where(row == column, 0.5, 0.0))
    ).astype(jnp.bfloat16)

    tile = (slices, width)
    z_of = side(tile, 0)
    lane = side(tile, 1)
    for load in loads[:-1]:
        load.wait()
    first = jnp.zeros(tile, jnp.int32)
    for z in range(slices):
        first = jnp.where(z_of == z, shear[z], first)
    support = [
        jnp.where(me * cells + b >= first, 1.0, 0.0).astype(jnp.float32) for b in range(cells)
    ]
    exit_rate = []
    for l in range(lines):
        for b in range(cells):
            total = conc[0, b] * exit_mu[l, 0]
            for e in range(1, elements):
                total += conc[e, b] * exit_mu[l, e]
            exit_rate.append(total * support[b])
    stacked = jnp.concatenate(exit_rate, axis=0)
    high = stacked.astype(jnp.bfloat16)
    low = (stacked - high.astype(jnp.float32)).astype(jnp.bfloat16)
    paths = jnp.dot(
        jnp.concatenate([high, low], axis=1), sums, preferred_element_type=jnp.float32
    )

    span = cells * rows
    used = (lines + 1) * chunk

    def part(j):
        return pl.ds(pl.multiple_of(j * rows, 8), rows)

    def put(target, step, q, value):
        for i in range(chunk):
            target[pl.ds(q * chunk + i, owners, stride=step), :] = value[
                i * owners : (i + 1) * owners
            ]

    def slab_copy(d, target):
        return pltpu.make_async_remote_copy(
            src_ref=slab_out,
            dst_ref=slab_in.at[d - 1],
            send_sem=slab_send.at[d - 1],
            recv_sem=slab_recv.at[d - 1],
            device_id={"beam": me, "gy": target},
            device_id_type=MESH,
        )

    def near_copy(d, j, target, source):
        return pltpu.make_async_remote_copy(
            src_ref=near_out.at[part(j)],
            dst_ref=near_in.at[d - 1, source],
            send_sem=near_send.at[d - 1, j],
            recv_sem=near_recv.at[d - 1, source],
            device_id={"beam": j * stride, "gy": target},
            device_id_type=MESH,
        )

    def out_copy(j, target, source, tiles):
        size = tiles * rows
        return pltpu.make_async_remote_copy(
            src_ref=sent.at[pl.ds(pl.multiple_of(j * span, 8), size)],
            dst_ref=taken.at[source, pl.ds(0, size)],
            send_sem=out_send.at[j],
            recv_sem=out_recv.at[source],
            device_id={"beam": target},
            device_id_type=MESH,
        )

    def back_copy(j, target):
        return pltpu.make_async_remote_copy(
            src_ref=reply.at[target],
            dst_ref=back.at[part(j)],
            send_sem=back_send.at[target],
            recv_sem=back_recv.at[j],
            device_id={"beam": target},
            device_id_type=MESH,
        )

    @pl.when(slab > 0)
    def _():
        put(near_out, rows, 0, jnp.ones(tile, jnp.float32))
        for r in range(used, rows):
            near_out[pl.ds(r, owners, stride=rows), :] = jnp.zeros((owners, width), jnp.float32)
        for l in range(lines):
            packed = jnp.zeros(tile, jnp.float32)
            for b in range(cells):
                c = l * cells + b
                packed = jnp.where(lane == b, paths[c * slices : (c + 1) * slices, width:], packed)
            passed = jnp.exp(-packed)
            slab_out[l] = passed
            put(near_out, rows, l + 1, passed)
        wait_barrier()
        for d in range(1, slabs):

            @pl.when(slab >= d)
            def _(d=d):
                loop(owners, lambda j: near_copy(d, j, slab - d, me).start())
                slab_copy(d, slab - d).start()

    before = jnp.zeros(tile, jnp.float32)
    rates = []
    for b in range(cells):
        rate = conc[0, b] * incident_mu[0]
        for e in range(1, elements):
            rate += conc[e, b] * incident_mu[e]
        rate *= support[b]
        rates.append(rate)
        depth = before + 0.5 * rate
        before += rate
        for l in range(lines):
            c = l * cells + b
            path = paths[c * slices : (c + 1) * slices, :width]
            weight[c] = support[b] * jnp.exp(-(depth + path))

    for b in range(cells):
        for r in range(used, rows):
            sent[pl.ds(b * rows + r, owners, stride=span), :] = jnp.zeros(
                (owners, width), jnp.float32
            )

    @pl.when(slab < slabs - 1)
    def _():
        for b in range(cells):
            tiles = sent.at[pl.ds(b * rows, owners * span - b * rows)]
            put(tiles, span, 0, rates[b])
            for l in range(lines):
                put(tiles, span, l + 1, weight[l * cells + b] * conc[line[l], b])

        pl.when(slab == 0)(wait_barrier)
        other_owners(lambda j, s: out_copy(j, s, me, cells).start())

    @pl.when(slab == slabs - 1)
    def _():
        put(sent, span, 0, before)
        for l in range(lines):
            partial = weight[l * cells] * conc[line[l], 0]
            for b in range(1, cells):
                partial += weight[l * cells + b] * conc[line[l], b]
            put(sent, span, l + 1, partial)
        if slabs == 1:
            wait_barrier()
        other_owners(lambda j, s: out_copy(j, s, me, 1).start())

    loads[-1].wait()
    for l in range(lines):
        values = data[tilt[0], l]
        for i in range(chunk):
            measured[pl.ds((l + 1) * chunk + i, owners, stride=rows), :] = values[
                i * owners : (i + 1) * owners
            ]
    for r in list(range(chunk)) + list(range((lines + 1) * chunk, rows)):
        measured[pl.ds(r, owners, stride=rows), :] = jnp.zeros((owners, width), jnp.float32)

    def own():
        taken[me, 0:rows] = sent[pl.ds(pl.multiple_of(rank * span, 8), rows), :]

        @pl.when(slab < slabs - 1)
        def _():
            taken[me] = sent[pl.ds(pl.multiple_of(rank * span, 8), span), :]
            for d in range(1, slabs):

                @pl.when(slab + d < slabs)
                def _(d=d):
                    loop(bricks, lambda s: near_copy(d, rank, slab, s).wait_recv())

            other_bricks(lambda s: out_copy(rank, s, s, cells).wait_recv())

            def reduce(s):
                for d in range(1, slabs):

                    @pl.when(slab + d < slabs)
                    def _(d=d):
                        passed = near_in[d - 1, s]
                        for b in range(cells):
                            at = pl.ds(b * rows, rows)
                            taken[s, at] *= jnp.broadcast_to(passed[:, b : b + 1], (rows, width))

                total = taken[s, 0:rows]
                for b in range(1, cells):
                    total += taken[s, b * rows : (b + 1) * rows]
                taken[s, 0:rows] = total

            loop(bricks, reduce)

        @pl.when(slab == slabs - 1)
        def _():
            other_bricks(lambda s: out_copy(rank, s, s, 1).wait_recv())

        head = side((rows, width), 0) < chunk

        def one(s, carry):
            run, emission = carry
            start = jnp.where(head, run, 0.0)
            spread = start
            for q in range(1, lines + 1):
                spread += pltpu.roll(start, q * chunk, 0)
            passed = jnp.exp(-spread)
            reply[s] = passed
            values = taken[s, 0:rows]
            return run + values, emission + passed * values

        zero = jnp.zeros((rows, width), jnp.float32)
        _, emission = fold(bricks, one, (zero, zero))
        ratio = measured[part(rank), :] / emission

        def finish(s):
            reply[s] = jnp.where(head, reply[s], ratio)

        loop(bricks, finish)
        other_bricks(lambda s: back_copy(rank, s).start())
        back[part(rank), :] = reply[me]

    when(is_owner, own)
    for d in range(1, slabs):

        @pl.when(slab + d < slabs)
        def _(d=d):
            slab_copy(d, slab).wait_recv()
            for l in range(lines):
                for b in range(cells):
                    weight[l * cells + b] *= jnp.broadcast_to(
                        slab_in[d - 1, l][:, b : b + 1], tile
                    )

    other_owners(lambda j, s: back_copy(j, me).wait_recv())

    def get(q):
        return jnp.concatenate(
            [back[pl.ds(q * chunk + i, owners, stride=rows), :] for i in range(chunk)], axis=0
        )

    arrived = get(0)
    ratios = [get(l + 1) for l in range(lines)]
    same = [
        [jnp.where(line[l] == line[k], 1.0, 0.0).astype(jnp.float32) for k in range(lines)]
        for l in range(lines)
    ]
    for b in range(cells):
        kept = [weight[l * cells + b] * arrived for l in range(lines)]
        raised = [kept[l] * ratios[l] for l in range(lines)]
        factor = []
        for l in range(lines):
            top = blend_weight + raised[l]
            bottom = blend_weight + kept[l]
            for k in range(lines):
                if k != l:
                    top += same[l][k] * raised[k]
                    bottom += same[l][k] * kept[k]
            factor.append(top / bottom)
        for e in range(elements):
            scale = 1.0
            for l in range(lines):
                scale = jnp.where(line[l] == e, factor[l], scale)
            updated[e, b] = conc[e, b] * scale

    @pl.when(slab < slabs - 1)
    def _():
        other_owners(lambda j, s: out_copy(j, s, me, cells).wait_send())

    @pl.when(slab == slabs - 1)
    def _():
        other_owners(lambda j, s: out_copy(j, s, me, 1).wait_send())

    when(is_owner, lambda: other_bricks(lambda s: back_copy(rank, s).wait_send()))
    for d in range(1, slabs):

        @pl.when(slab >= d)
        def _(d=d):
            loop(owners, lambda j: near_copy(d, j, slab - d, me).wait_send())
            slab_copy(d, slab - d).wait_send()


def per_device(
    bricks, slabs, concentration, incident_mu, exit_mu, line_element, tilt_index, shear, data
):
    elements, cells, slices, width = concentration.shape
    lines = exit_mu.shape[0]
    owners, _, _, rows = layout(slices, bricks, lines)
    f32 = jnp.float32
    others = max(slabs - 1, 1)
    arguments = (concentration, incident_mu, exit_mu, line_element, tilt_index, shear, data)
    return pl.pallas_call(
        functools.partial(kernel, bricks, slabs),
        out_shape=pltpu.VMEM(concentration.shape, f32),
        in_specs=[pl.BlockSpec(memory_space=pl.ANY)] * 7,
        out_specs=pl.BlockSpec(memory_space=pltpu.VMEM),
        scratch_shapes=[
            pltpu.VMEM(concentration.shape, f32),
            pltpu.VMEM(data.shape, f32),
            pltpu.SMEM(incident_mu.shape, f32),
            pltpu.SMEM(exit_mu.shape, f32),
            pltpu.SMEM(line_element.shape, jnp.int32),
            pltpu.SMEM(tilt_index.shape, jnp.int32),
            pltpu.SMEM(shear.shape, jnp.int32),
            pltpu.VMEM((lines * cells, slices, width), f32),
            pltpu.VMEM((lines, slices, width), f32),
            pltpu.VMEM((others, lines, slices, width), f32),
            pltpu.VMEM((owners * rows, width), f32),
            pltpu.VMEM((others, bricks, rows, width), f32),
            pltpu.VMEM((owners * cells * rows, width), f32),
            pltpu.VMEM((bricks, cells * rows, width), f32),
            pltpu.VMEM((bricks, rows, width), f32),
            pltpu.VMEM((owners * rows, width), f32),
            pltpu.VMEM((owners * rows, width), f32),
            pltpu.SemaphoreType.DMA((7,)),
            pltpu.SemaphoreType.DMA((others,)),
            pltpu.SemaphoreType.DMA((others,)),
            pltpu.SemaphoreType.DMA((others, owners)),
            pltpu.SemaphoreType.DMA((others, bricks)),
            pltpu.SemaphoreType.DMA((owners,)),
            pltpu.SemaphoreType.DMA((bricks,)),
            pltpu.SemaphoreType.DMA((bricks,)),
            pltpu.SemaphoreType.DMA((owners,)),
        ],
        compiler_params=pltpu.CompilerParams(
            collective_id=0, has_side_effects=True, vmem_limit_bytes=16 * 1024 * 1024
        ),
        name="update",
    )(*(x if x.size == 1 else pltpu.with_memory_space_constraint(x, pltpu.HBM) for x in arguments))


def solution(mesh):
    placed = (
        P("grp", "beam", None, "gy"),
        P(),
        P(),
        P(),
        P(),
        P("grp"),
        P("grp", None, None, "gy"),
    )
    return jax.shard_map(
        functools.partial(per_device, mesh.shape["beam"], mesh.shape["gy"]),
        mesh=mesh,
        in_specs=placed,
        out_specs=P("grp", "beam", None, "gy"),
        check_vma=False,
    )
```

```python
import functools

import jax
import jax.numpy as jnp
from jax import lax
from jax.experimental import pallas as pl
from jax.experimental.pallas import tpu as pltpu
from jax.sharding import PartitionSpec as P

blend_weight = 0.05
MESH = pl.DeviceIdType.MESH


def loop(count, body):
    if count <= 16:
        for step in range(count):
            body(step)
    else:

        def one(step, carry):
            body(step)
            return carry

        lax.fori_loop(0, count, one, 0)


def fold(count, body, carry):
    if count <= 16:
        for step in range(count):
            carry = body(step, carry)
        return carry
    return lax.fori_loop(0, count, body, carry)


def layout(slices, bricks, lines):
    owners = min(slices, bricks)
    while slices % owners or bricks % owners:
        owners -= 1
    chunk = slices // owners
    rows = -(-(lines + 1) * chunk // 8) * 8
    return owners, bricks // owners, chunk, rows


def kernel(
    bricks,
    slabs,
    conc_hbm,
    incident_hbm,
    exit_hbm,
    line_hbm,
    tilt_hbm,
    shear_hbm,
    data_hbm,
    updated,
    conc,
    data,
    incident_mu,
    exit_mu,
    line,
    tilt,
    shear,
    weight,
    slab_out,
    slab_in,
    sent,
    taken,
    reply,
    back,
    measured,
    load_sem,
    slab_send,
    slab_recv,
    out_send,
    out_recv,
    back_send,
    back_recv,
):
    elements, cells, slices, width = conc.shape
    lines = exit_mu.shape[0]
    owners, stride, chunk, rows = layout(slices, bricks, lines)
    me = lax.axis_index("beam")
    slab = lax.axis_index("gy")
    rank = me if stride == 1 else me // stride
    is_owner = True if stride == 1 else lax.rem(me, stride) == 0

    loads = [
        pltpu.make_async_copy(src, dst, load_sem.at[k])
        for k, (src, dst) in enumerate(
            (
                (conc_hbm, conc),
                (exit_hbm, exit_mu),
                (shear_hbm, shear),
                (incident_hbm, incident_mu),
                (line_hbm, line),
                (tilt_hbm, tilt),
                (data_hbm, data),
            )
        )
    ]
    for load in loads:
        load.start()

    def when(condition, body):
        if condition is True:
            body()
        else:
            pl.when(condition)(body)

    def other_bricks(body):
        if bricks <= 16:
            for k in sorted(range(1, bricks), key=lambda k: abs(2 * k - bricks)):
                body(lax.rem(me + k, bricks))
        else:
            loop(bricks, lambda s: pl.when(s != me)(lambda: body(s)))

    def other_owners(body):
        if stride == 1:
            other_bricks(lambda s: body(s, s))
        else:
            loop(owners, lambda j: pl.when(j * stride != me)(lambda: body(j, j * stride)))

    barrier = pltpu.get_barrier_semaphore()

    def greet_brick(s):
        pl.semaphore_signal(barrier, inc=1, device_id={"beam": s}, device_id_type=MESH)

    def greet_owner(j, s):
        greet_brick(s)

    for d in range(1, slabs):
        pl.semaphore_signal(
            barrier,
            inc=1,
            device_id={"gy": lax.rem(slab + d, slabs)},
            device_id_type=MESH,
        )
    if stride == 1:
        other_bricks(greet_brick)
    else:
        pl.when(is_owner)(lambda: other_bricks(greet_brick))
        pl.when(jnp.logical_not(is_owner))(lambda: other_owners(greet_owner))

    def side(shape, axis):
        return lax.broadcasted_iota(jnp.int32, shape, axis)

    square = (2 * width, 2 * width)
    row = lax.rem(side(square, 0), width)
    column = side(square, 1)
    sums = jnp.where(
        column >= width, 1.0, jnp.where(row > column, 1.0, jnp.where(row == column, 0.5, 0.0))
    ).astype(jnp.bfloat16)

    tile = (slices, width)
    z_of = side(tile, 0)
    lane = side(tile, 1)
    for load in loads[:-1]:
        load.wait()
    first = jnp.zeros(tile, jnp.int32)
    for z in range(slices):
        first = jnp.where(z_of == z, shear[z], first)
    support = [
        jnp.where(me * cells + b >= first, 1.0, 0.0).astype(jnp.float32) for b in range(cells)
    ]
    exit_rate = []
    for l in range(lines):
        for b in range(cells):
            total = conc[0, b] * exit_mu[l, 0]
            for e in range(1, elements):
                total += conc[e, b] * exit_mu[l, e]
            exit_rate.append(total * support[b])
    stacked = jnp.concatenate(exit_rate, axis=0)
    high = stacked.astype(jnp.bfloat16)
    low = (stacked - high.astype(jnp.float32)).astype(jnp.bfloat16)
    paths = jnp.dot(
        jnp.concatenate([high, low], axis=1), sums, preferred_element_type=jnp.float32
    )

    packed = jnp.zeros(tile, jnp.float32)
    for c in range(lines * cells):
        packed = jnp.where(lane == c, paths[c * slices : (c + 1) * slices, width:], packed)
    slab_out[...] = packed

    def slab_copy(d, target):
        return pltpu.make_async_remote_copy(
            src_ref=slab_out,
            dst_ref=slab_in.at[d - 1],
            send_sem=slab_send.at[d - 1],
            recv_sem=slab_recv.at[d - 1],
            device_id={"gy": target},
            device_id_type=MESH,
        )

    if stride == 1:
        pl.semaphore_wait(barrier, bricks - 1 + slabs - 1)
    else:
        pl.when(is_owner)(lambda: pl.semaphore_wait(barrier, bricks - 1 + slabs - 1))
        pl.when(jnp.logical_not(is_owner))(
            lambda: pl.semaphore_wait(barrier, owners + slabs - 1)
        )
    for d in range(1, slabs):
        pl.when(slab >= d)(lambda d=d: slab_copy(d, slab - d).start())

    before = jnp.zeros(tile, jnp.float32)
    for b in range(cells):
        rate = conc[0, b] * incident_mu[0]
        for e in range(1, elements):
            rate += conc[e, b] * incident_mu[e]
        rate *= support[b]
        depth = before + 0.5 * rate
        before += rate
        for l in range(lines):
            c = l * cells + b
            path = paths[c * slices : (c + 1) * slices, :width]
            weight[c] = support[b] * jnp.exp(-(depth + path))

    def put(q, value):
        for i in range(chunk):
            sent[pl.ds(q * chunk + i, owners, stride=rows), :] = value[
                i * owners : (i + 1) * owners
            ]

    put(0, before)
    if rows > (lines + 1) * chunk:
        for r in range((lines + 1) * chunk, rows):
            sent[pl.ds(r, owners, stride=rows), :] = jnp.zeros((owners, width), jnp.float32)

    for d in range(1, slabs):

        @pl.when(slab + d < slabs)
        def _(d=d):
            slab_copy(d, slab - d).wait_recv()
            passed = jnp.exp(-slab_in[d - 1])
            for c in range(lines * cells):
                weight[c] *= jnp.broadcast_to(passed[:, c : c + 1], tile)

    for l in range(lines):
        source = line[l]
        partial = weight[l * cells] * conc[source, 0]
        for b in range(1, cells):
            partial += weight[l * cells + b] * conc[source, b]
        put(l + 1, partial)

    def part(j):
        start = j * rows
        return pl.ds(start if isinstance(j, int) else pl.multiple_of(start, 8), rows)

    def out_copy(j, target, source):
        return pltpu.make_async_remote_copy(
            src_ref=sent.at[part(j)],
            dst_ref=taken.at[part(source)],
            send_sem=out_send,
            recv_sem=out_recv,
            device_id={"beam": target},
            device_id_type=MESH,
        )

    def back_copy(j, target):
        return pltpu.make_async_remote_copy(
            src_ref=reply.at[part(target)],
            dst_ref=back.at[part(j)],
            send_sem=back_send,
            recv_sem=back_recv,
            device_id={"beam": target},
            device_id_type=MESH,
        )

    def all_of(ref, count, send_sem, recv_sem):
        whole = ref.at[pl.ds(0, count * rows)]
        return pltpu.make_async_remote_copy(
            src_ref=whole,
            dst_ref=whole,
            send_sem=send_sem,
            recv_sem=recv_sem,
            device_id={"beam": lax.rem(me + 1, bricks)},
            device_id_type=MESH,
        )

    def with_owners(body):
        when(is_owner, lambda: body(owners - 1))
        if stride > 1:
            pl.when(jnp.logical_not(is_owner))(lambda: body(owners))

    other_owners(lambda j, s: out_copy(j, s, me).start())

    loads[-1].wait()
    for l in range(lines):
        values = data[tilt[0], l]
        for i in range(chunk):
            measured[pl.ds((l + 1) * chunk + i, owners, stride=rows), :] = values[
                i * owners : (i + 1) * owners
            ]
    for r in list(range(chunk)) + list(range((lines + 1) * chunk, rows)):
        measured[pl.ds(r, owners, stride=rows), :] = jnp.zeros((owners, width), jnp.float32)

    def own():
        taken[part(me), :] = sent[part(rank), :]
        all_of(taken, bricks - 1, out_send, out_recv).wait_recv()
        head = side((rows, width), 0) < chunk

        def one(s, carry):
            run, emission = carry
            start = jnp.where(head, run, 0.0)
            spread = start
            for q in range(1, lines + 1):
                spread += pltpu.roll(start, q * chunk, 0)
            passed = jnp.exp(-spread)
            reply[part(s), :] = passed
            values = taken[part(s), :]
            return run + values, emission + passed * values

        zero = jnp.zeros((rows, width), jnp.float32)
        _, emission = fold(bricks, one, (zero, zero))
        ratio = measured[part(rank), :] / emission

        def finish(s):
            reply[part(s), :] = jnp.where(head, reply[part(s), :], ratio)

        loop(bricks, finish)
        other_bricks(lambda s: back_copy(rank, s).start())
        back[part(rank), :] = reply[part(me), :]

    when(is_owner, own)
    with_owners(lambda count: all_of(back, count, back_send, back_recv).wait_recv())

    def get(q):
        return jnp.concatenate(
            [back[pl.ds(q * chunk + i, owners, stride=rows), :] for i in range(chunk)], axis=0
        )

    arrived = get(0)
    ratios = [get(l + 1) for l in range(lines)]
    same = [
        [jnp.where(line[l] == line[k], 1.0, 0.0).astype(jnp.float32) for k in range(lines)]
        for l in range(lines)
    ]
    for b in range(cells):
        kept = [weight[l * cells + b] * arrived for l in range(lines)]
        raised = [kept[l] * ratios[l] for l in range(lines)]
        factor = []
        for l in range(lines):
            top = blend_weight + raised[l]
            bottom = blend_weight + kept[l]
            for k in range(lines):
                if k != l:
                    top += same[l][k] * raised[k]
                    bottom += same[l][k] * kept[k]
            factor.append(top / bottom)
        for e in range(elements):
            scale = 1.0
            for l in range(lines):
                scale = jnp.where(line[l] == e, factor[l], scale)
            updated[e, b] = conc[e, b] * scale

    with_owners(lambda count: all_of(sent, count, out_send, out_recv).wait_send())
    when(is_owner, lambda: all_of(reply, bricks - 1, back_send, back_recv).wait_send())
    for d in range(1, slabs):
        pl.when(slab >= d)(lambda d=d: slab_copy(d, slab - d).wait_send())


def per_device(
    bricks, slabs, concentration, incident_mu, exit_mu, line_element, tilt_index, shear, data
):
    elements, cells, slices, width = concentration.shape
    lines = exit_mu.shape[0]
    owners, _, _, rows = layout(slices, bricks, lines)
    f32 = jnp.float32
    arguments = (concentration, incident_mu, exit_mu, line_element, tilt_index, shear, data)
    return pl.pallas_call(
        functools.partial(kernel, bricks, slabs),
        out_shape=pltpu.VMEM(concentration.shape, f32),
        in_specs=[pl.BlockSpec(memory_space=pl.ANY)] * 7,
        out_specs=pl.BlockSpec(memory_space=pltpu.VMEM),
        scratch_shapes=[
            pltpu.VMEM(concentration.shape, f32),
            pltpu.VMEM(data.shape, f32),
            pltpu.SMEM(incident_mu.shape, f32),
            pltpu.SMEM(exit_mu.shape, f32),
            pltpu.SMEM(line_element.shape, jnp.int32),
            pltpu.SMEM(tilt_index.shape, jnp.int32),
            pltpu.SMEM(shear.shape, jnp.int32),
            pltpu.VMEM((lines * cells, slices, width), f32),
            pltpu.VMEM((slices, width), f32),
            pltpu.VMEM((max(slabs - 1, 1), slices, width), f32),
            pltpu.VMEM((owners * rows, width), f32),
            pltpu.VMEM((bricks * rows, width), f32),
            pltpu.VMEM((bricks * rows, width), f32),
            pltpu.VMEM((owners * rows, width), f32),
            pltpu.VMEM((owners * rows, width), f32),
            pltpu.SemaphoreType.DMA((7,)),
            pltpu.SemaphoreType.DMA((max(slabs - 1, 1),)),
            pltpu.SemaphoreType.DMA((max(slabs - 1, 1),)),
            pltpu.SemaphoreType.DMA,
            pltpu.SemaphoreType.DMA,
            pltpu.SemaphoreType.DMA,
            pltpu.SemaphoreType.DMA,
        ],
        compiler_params=pltpu.CompilerParams(
            collective_id=0, has_side_effects=True, vmem_limit_bytes=16 * 1024 * 1024
        ),
        name="update",
    )(*(x if x.size == 1 else pltpu.with_memory_space_constraint(x, pltpu.HBM) for x in arguments))


def solution(mesh):
    placed = (
        P("grp", "beam", None, "gy"),
        P(),
        P(),
        P(),
        P(),
        P("grp"),
        P("grp", None, None, "gy"),
    )
    return jax.shard_map(
        functools.partial(per_device, mesh.shape["beam"], mesh.shape["gy"]),
        mesh=mesh,
        in_specs=placed,
        out_specs=P("grp", "beam", None, "gy"),
        check_vma=False,
    )
```

```python
import functools

import jax
import jax.numpy as jnp
from jax import lax
from jax.experimental import pallas as pl
from jax.experimental.pallas import tpu as pltpu
from jax.sharding import PartitionSpec as P

blend_weight = 0.05
MESH = pl.DeviceIdType.MESH


def loop(count, body):
    if count <= 16:
        for step in range(count):
            body(step)
    else:

        def one(step, carry):
            body(step)
            return carry

        lax.fori_loop(0, count, one, 0)


def fold(count, body, carry):
    if count <= 16:
        for step in range(count):
            carry = body(step, carry)
        return carry
    return lax.fori_loop(0, count, body, carry)


def layout(slices, bricks, lines):
    owners = min(slices, bricks)
    while slices % owners or bricks % owners:
        owners -= 1
    chunk = slices // owners
    rows = -(-(lines + 1) * chunk // 8) * 8
    return owners, bricks // owners, chunk, rows


def kernel(
    bricks,
    slabs,
    conc_hbm,
    incident_hbm,
    exit_hbm,
    line_hbm,
    tilt_hbm,
    shear_hbm,
    data_hbm,
    updated,
    conc,
    data,
    incident_mu,
    exit_mu,
    line,
    tilt,
    shear,
    sums,
    weight,
    slab_out,
    slab_in,
    sent,
    taken,
    reply,
    back,
    measured,
    load_sem,
    slab_send,
    slab_recv,
    out_send,
    out_recv,
    back_send,
    back_recv,
    go,
):
    elements, cells, slices, width = conc.shape
    lines = exit_mu.shape[0]
    owners, stride, chunk, rows = layout(slices, bricks, lines)
    me = lax.axis_index("beam")
    slab = lax.axis_index("gy")
    rank = me if stride == 1 else me // stride
    is_owner = True if stride == 1 else lax.rem(me, stride) == 0

    loads = [
        pltpu.make_async_copy(src, dst, load_sem.at[k])
        for k, (src, dst) in enumerate(
            (
                (conc_hbm, conc),
                (exit_hbm, exit_mu),
                (shear_hbm, shear),
                (incident_hbm, incident_mu),
                (line_hbm, line),
                (tilt_hbm, tilt),
                (data_hbm, data),
            )
        )
    ]
    for load in loads[:-1]:
        load.start()

    def when(condition, body):
        if condition is True:
            body()
        else:
            pl.when(condition)(body)

    def other_bricks(body):
        if bricks <= 16:
            for k in sorted(range(1, bricks), key=lambda k: abs(2 * k - bricks)):
                body(lax.rem(me + k, bricks))
        else:
            loop(bricks, lambda s: pl.when(s != me)(lambda: body(s)))

    def other_owners(body):
        if stride == 1:
            other_bricks(lambda s: body(s, s))
        else:
            loop(owners, lambda j: pl.when(j * stride != me)(lambda: body(j, j * stride)))

    barrier = pltpu.get_barrier_semaphore()

    def greet(brick, place):
        pl.semaphore_signal(
            barrier, inc=1, device_id={"beam": brick, "gy": place}, device_id_type=MESH
        )

    for d in range(1, slabs):
        pl.when(slab + d < slabs)(lambda d=d: greet(me, slab + d))
    pl.when(slab > 0)(lambda: greet(me, 0))

    def greet_slab(body):
        when(is_owner, lambda: other_bricks(lambda s: body(s)))
        if stride > 1:
            pl.when(jnp.logical_not(is_owner))(lambda: other_owners(lambda j, s: body(s)))

    greet_slab(lambda s: greet(s, 0))

    def first_slab():
        when(
            is_owner, lambda: pl.semaphore_wait(barrier, slabs * (bricks - 1) + slabs - 1)
        )
        if stride > 1:
            pl.when(jnp.logical_not(is_owner))(
                lambda: pl.semaphore_wait(barrier, slabs * owners + slabs - 1)
            )
        for d in range(1, slabs):
            pl.semaphore_signal(
                go, inc=1, device_id={"beam": me, "gy": slab + d}, device_id_type=MESH
            )

    def side(shape, axis):
        return lax.broadcasted_iota(jnp.int32, shape, axis)

    square = (2 * width, 2 * width)
    row = lax.rem(side(square, 0), width)
    column = side(square, 1)
    sums[...] = jnp.where(
        column >= width, 1.0, jnp.where(row > column, 1.0, jnp.where(row == column, 0.5, 0.0))
    ).astype(jnp.bfloat16)

    tile = (slices, width)
    z_of = side(tile, 0)
    lane = side(tile, 1)
    for load in loads[1:-1]:
        load.wait()
    mu = [[exit_mu[l, e] for e in range(elements)] for l in range(lines)]
    mu_in = [incident_mu[e] for e in range(elements)]
    emitter = [line[l] for l in range(lines)]
    first = jnp.zeros(tile, jnp.int32)
    for z in range(slices):
        first = jnp.where(z_of == z, shear[z], first)
    support = [
        jnp.where(me * cells + b >= first, 1.0, 0.0).astype(jnp.float32) for b in range(cells)
    ]
    loads[0].wait()
    loads[-1].start()
    exit_rate = []
    for l in range(lines):
        for b in range(cells):
            total = conc[0, b] * mu[l][0]
            for e in range(1, elements):
                total += conc[e, b] * mu[l][e]
            exit_rate.append(total * support[b])
    stacked = jnp.concatenate(exit_rate, axis=0)
    high = stacked.astype(jnp.bfloat16)
    low = (stacked - high.astype(jnp.float32)).astype(jnp.bfloat16)
    paths = jnp.dot(
        jnp.concatenate([high, low], axis=1), sums[...], preferred_element_type=jnp.float32
    )

    packed = jnp.zeros(tile, jnp.float32)
    for c in range(lines * cells):
        packed = jnp.where(lane == c, paths[c * slices : (c + 1) * slices, width:], packed)
    slab_out[...] = packed

    def slab_copy(d, target):
        return pltpu.make_async_remote_copy(
            src_ref=slab_out,
            dst_ref=slab_in.at[d - 1],
            send_sem=slab_send.at[d - 1],
            recv_sem=slab_recv.at[d - 1],
            device_id={"gy": target},
            device_id_type=MESH,
        )

    for g in range(1, slabs):
        pl.when(slab == g)(lambda g=g: pl.semaphore_wait(barrier, g))
    for d in range(1, slabs):
        pl.when(slab >= d)(lambda d=d: slab_copy(d, slab - d).start())

    before = jnp.zeros(tile, jnp.float32)
    for b in range(cells):
        rate = conc[0, b] * mu_in[0]
        for e in range(1, elements):
            rate += conc[e, b] * mu_in[e]
        rate *= support[b]
        depth = before + 0.5 * rate
        before += rate
        for l in range(lines):
            c = l * cells + b
            path = paths[c * slices : (c + 1) * slices, :width]
            weight[c] = support[b] * jnp.exp(-(depth + path))

    def put(q, value):
        for i in range(chunk):
            sent[pl.ds(q * chunk + i, owners, stride=rows), :] = value[
                i * owners : (i + 1) * owners
            ]

    pl.when(slab == 0)(first_slab)
    put(0, before)
    if rows > (lines + 1) * chunk:
        for r in range((lines + 1) * chunk, rows):
            sent[pl.ds(r, owners, stride=rows), :] = jnp.zeros((owners, width), jnp.float32)

    for d in range(1, slabs):

        @pl.when(slab + d < slabs)
        def _(d=d):
            slab_copy(d, slab - d).wait_recv()
            passed = jnp.exp(-slab_in[d - 1])
            for c in range(lines * cells):
                weight[c] *= jnp.broadcast_to(passed[:, c : c + 1], tile)

    for l in range(lines):
        source = emitter[l]
        partial = weight[l * cells] * conc[source, 0]
        for b in range(1, cells):
            partial += weight[l * cells + b] * conc[source, b]
        put(l + 1, partial)

    def part(j):
        start = j * rows
        return pl.ds(start if isinstance(j, int) else pl.multiple_of(start, 8), rows)

    def out_copy(j, target, source):
        return pltpu.make_async_remote_copy(
            src_ref=sent.at[part(j)],
            dst_ref=taken.at[part(source)],
            send_sem=out_send,
            recv_sem=out_recv,
            device_id={"beam": target},
            device_id_type=MESH,
        )

    def back_copy(j, target):
        return pltpu.make_async_remote_copy(
            src_ref=reply.at[part(target)],
            dst_ref=back.at[part(j)],
            send_sem=back_send,
            recv_sem=back_recv,
            device_id={"beam": target},
            device_id_type=MESH,
        )

    def all_of(ref, count, send_sem, recv_sem):
        whole = ref.at[pl.ds(0, count * rows)]
        return pltpu.make_async_remote_copy(
            src_ref=whole,
            dst_ref=whole,
            send_sem=send_sem,
            recv_sem=recv_sem,
            device_id={"beam": lax.rem(me + 1, bricks)},
            device_id_type=MESH,
        )

    def with_owners(body):
        when(is_owner, lambda: body(owners - 1))
        if stride > 1:
            pl.when(jnp.logical_not(is_owner))(lambda: body(owners))

    if slabs > 1:
        pl.when(slab > 0)(lambda: pl.semaphore_wait(go, 1))
    other_owners(lambda j, s: out_copy(j, s, me).start())

    loads[-1].wait()
    for l in range(lines):
        values = data[tilt[0], l]
        for i in range(chunk):
            measured[pl.ds((l + 1) * chunk + i, owners, stride=rows), :] = values[
                i * owners : (i + 1) * owners
            ]
    for r in list(range(chunk)) + list(range((lines + 1) * chunk, rows)):
        measured[pl.ds(r, owners, stride=rows), :] = jnp.zeros((owners, width), jnp.float32)

    def own():
        taken[part(me), :] = sent[part(rank), :]
        all_of(taken, bricks - 1, out_send, out_recv).wait_recv()
        head = side((rows, width), 0) < chunk

        def one(s, carry):
            run, emission = carry
            start = jnp.where(head, run, 0.0)
            spread = start
            for q in range(1, lines + 1):
                spread += pltpu.roll(start, q * chunk, 0)
            passed = jnp.exp(-spread)
            reply[part(s), :] = passed
            values = taken[part(s), :]
            return run + values, emission + passed * values

        zero = jnp.zeros((rows, width), jnp.float32)
        _, emission = fold(bricks, one, (zero, zero))
        ratio = measured[part(rank), :] / emission

        def finish(s):
            reply[part(s), :] = jnp.where(head, reply[part(s), :], ratio)

        loop(bricks, finish)
        other_bricks(lambda s: back_copy(rank, s).start())
        back[part(rank), :] = reply[part(me), :]

    when(is_owner, own)
    with_owners(lambda count: all_of(back, count, back_send, back_recv).wait_recv())

    def get(q):
        return jnp.concatenate(
            [back[pl.ds(q * chunk + i, owners, stride=rows), :] for i in range(chunk)], axis=0
        )

    arrived = get(0)
    ratios = [get(l + 1) for l in range(lines)]
    same = [
        [jnp.where(emitter[l] == emitter[k], 1.0, 0.0).astype(jnp.float32) for k in range(lines)]
        for l in range(lines)
    ]
    hit = [[emitter[l] == e for e in range(elements)] for l in range(lines)]
    for b in range(cells):
        kept = [weight[l * cells + b] * arrived for l in range(lines)]
        raised = [kept[l] * ratios[l] for l in range(lines)]
        factor = []
        for l in range(lines):
            top = blend_weight + raised[l]
            bottom = blend_weight + kept[l]
            for k in range(lines):
                if k != l:
                    top += same[l][k] * raised[k]
                    bottom += same[l][k] * kept[k]
            factor.append(top / bottom)
        for e in range(elements):
            scale = 1.0
            for l in range(lines):
                scale = jnp.where(hit[l][e], factor[l], scale)
            updated[e, b] = conc[e, b] * scale

    with_owners(lambda count: all_of(sent, count, out_send, out_recv).wait_send())
    when(is_owner, lambda: all_of(reply, bricks - 1, back_send, back_recv).wait_send())
    for d in range(1, slabs):
        pl.when(slab >= d)(lambda d=d: slab_copy(d, slab - d).wait_send())


def per_device(
    bricks, slabs, concentration, incident_mu, exit_mu, line_element, tilt_index, shear, data
):
    elements, cells, slices, width = concentration.shape
    lines = exit_mu.shape[0]
    owners, _, _, rows = layout(slices, bricks, lines)
    f32 = jnp.float32
    arguments = (concentration, incident_mu, exit_mu, line_element, tilt_index, shear, data)
    return pl.pallas_call(
        functools.partial(kernel, bricks, slabs),
        out_shape=pltpu.VMEM(concentration.shape, f32),
        in_specs=[pl.BlockSpec(memory_space=pl.ANY)] * 7,
        out_specs=pl.BlockSpec(memory_space=pltpu.VMEM),
        scratch_shapes=[
            pltpu.VMEM(concentration.shape, f32),
            pltpu.VMEM(data.shape, f32),
            pltpu.SMEM(incident_mu.shape, f32),
            pltpu.SMEM(exit_mu.shape, f32),
            pltpu.SMEM(line_element.shape, jnp.int32),
            pltpu.SMEM(tilt_index.shape, jnp.int32),
            pltpu.SMEM(shear.shape, jnp.int32),
            pltpu.VMEM((2 * width, 2 * width), jnp.bfloat16),
            pltpu.VMEM((lines * cells, slices, width), f32),
            pltpu.VMEM((slices, width), f32),
            pltpu.VMEM((max(slabs - 1, 1), slices, width), f32),
            pltpu.VMEM((owners * rows, width), f32),
            pltpu.VMEM((bricks * rows, width), f32),
            pltpu.VMEM((bricks * rows, width), f32),
            pltpu.VMEM((owners * rows, width), f32),
            pltpu.VMEM((owners * rows, width), f32),
            pltpu.SemaphoreType.DMA((7,)),
            pltpu.SemaphoreType.DMA((max(slabs - 1, 1),)),
            pltpu.SemaphoreType.DMA((max(slabs - 1, 1),)),
            pltpu.SemaphoreType.DMA,
            pltpu.SemaphoreType.DMA,
            pltpu.SemaphoreType.DMA,
            pltpu.SemaphoreType.DMA,
            pltpu.SemaphoreType.REGULAR,
        ],
        compiler_params=pltpu.CompilerParams(
            collective_id=0, has_side_effects=True, vmem_limit_bytes=16 * 1024 * 1024
        ),
        name="update",
    )(*(x if x.size == 1 else pltpu.with_memory_space_constraint(x, pltpu.HBM) for x in arguments))


def solution(mesh):
    placed = (
        P("grp", "beam", None, "gy"),
        P(),
        P(),
        P(),
        P(),
        P("grp"),
        P("grp", None, None, "gy"),
    )
    return jax.shard_map(
        functools.partial(per_device, mesh.shape["beam"], mesh.shape["gy"]),
        mesh=mesh,
        in_specs=placed,
        out_specs=P("grp", "beam", None, "gy"),
        check_vma=False,
    )
```

```python
import functools

import jax
import jax.numpy as jnp
from jax import lax
from jax.experimental import pallas as pl
from jax.experimental.pallas import tpu as pltpu
from jax.sharding import PartitionSpec as P

blend_weight = 0.05
MESH = pl.DeviceIdType.MESH


def over(start, stop, body, carry=0):
    if stop - start <= 16:
        for step in range(start, stop):
            carry = body(step, carry)
        return carry
    return lax.fori_loop(start, stop, body, carry)


def kernel(
    bricks,
    slabs,
    conc_hbm,
    incident_hbm,
    exit_hbm,
    line_hbm,
    tilt_hbm,
    shear_hbm,
    data_hbm,
    updated,
    conc,
    data,
    incident_mu,
    exit_mu,
    line,
    tilt,
    shear,
    sums,
    weight,
    slab_out,
    slab_in,
    sent,
    taken,
    passed_out,
    passed_in,
    ratios,
    load_sem,
    slab_send,
    slab_recv,
    out_send,
    out_recv,
    passed_send,
    passed_recv,
    ratio_send,
    ratio_recv,
):
    elements, cells, slices, width = conc.shape
    lines = exit_mu.shape[0]
    me = lax.axis_index("beam")
    slab = lax.axis_index("gy")

    loads = [
        pltpu.make_async_copy(src, dst, load_sem.at[k])
        for k, (src, dst) in enumerate(
            (
                (conc_hbm, conc),
                (exit_hbm, exit_mu),
                (shear_hbm, shear),
                (incident_hbm, incident_mu),
                (line_hbm, line),
                (tilt_hbm, tilt),
                (data_hbm, data),
            )
        )
    ]
    for load in loads[:-1]:
        load.start()

    barrier = pltpu.get_barrier_semaphore()

    def greet(brick, place):
        pl.semaphore_signal(
            barrier, inc=1, device_id={"beam": brick, "gy": place}, device_id_type=MESH
        )

    for d in range(1, slabs):
        pl.when(slab + d < slabs)(lambda d=d: greet(me, slab + d))

    @pl.when(me == 0)
    def _():
        def one(n, carry):
            greet(n, slab)
            return carry

        over(1, bricks, one)
        loads[-1].start()

    pl.when(me > 0)(lambda: greet(0, slab))

    def side(shape, axis):
        return lax.broadcasted_iota(jnp.int32, shape, axis)

    square = (2 * width, 2 * width)
    row = lax.rem(side(square, 0), width)
    column = side(square, 1)
    sums[...] = jnp.where(
        column >= width, 1.0, jnp.where(row > column, 1.0, jnp.where(row == column, 0.5, 0.0))
    ).astype(jnp.bfloat16)

    tile = (slices, width)
    z_of = side(tile, 0)
    lane = side(tile, 1)
    for load in loads[1:-1]:
        load.wait()
    mu = [[exit_mu[l, e] for e in range(elements)] for l in range(lines)]
    mu_in = [incident_mu[e] for e in range(elements)]
    emitter = [line[l] for l in range(lines)]
    first = jnp.zeros(tile, jnp.int32)
    for z in range(slices):
        first = jnp.where(z_of == z, shear[z], first)
    support = [
        jnp.where(me * cells + b >= first, 1.0, 0.0).astype(jnp.float32) for b in range(cells)
    ]
    loads[0].wait()
    exit_rate = []
    for l in range(lines):
        for b in range(cells):
            total = conc[0, b] * mu[l][0]
            for e in range(1, elements):
                total += conc[e, b] * mu[l][e]
            exit_rate.append(total * support[b])
    stacked = jnp.concatenate(exit_rate, axis=0)
    high = stacked.astype(jnp.bfloat16)
    low = (stacked - high.astype(jnp.float32)).astype(jnp.bfloat16)
    paths = jnp.dot(
        jnp.concatenate([high, low], axis=1), sums[...], preferred_element_type=jnp.float32
    )

    packed = jnp.zeros(tile, jnp.float32)
    for c in range(lines * cells):
        packed = jnp.where(lane == c, paths[c * slices : (c + 1) * slices, width:], packed)
    slab_out[...] = packed

    def slab_copy(d, target):
        return pltpu.make_async_remote_copy(
            src_ref=slab_out,
            dst_ref=slab_in.at[d - 1],
            send_sem=slab_send.at[d - 1],
            recv_sem=slab_recv.at[d - 1],
            device_id={"gy": target},
            device_id_type=MESH,
        )

    pl.when(me == 0)(lambda: pl.semaphore_wait(barrier, bricks - 1 + slab))
    pl.when(me > 0)(lambda: pl.semaphore_wait(barrier, 1 + slab))
    for d in range(1, slabs):
        pl.when(slab >= d)(lambda d=d: slab_copy(d, slab - d).start())

    before = jnp.zeros(tile, jnp.float32)
    for b in range(cells):
        rate = conc[0, b] * mu_in[0]
        for e in range(1, elements):
            rate += conc[e, b] * mu_in[e]
        rate *= support[b]
        depth = before + 0.5 * rate
        before += rate
        for l in range(lines):
            c = l * cells + b
            path = paths[c * slices : (c + 1) * slices, :width]
            weight[c] = support[b] * jnp.exp(-(depth + path))

    sent[0] = before

    for d in range(1, slabs):

        @pl.when(slab + d < slabs)
        def _(d=d):
            slab_copy(d, slab).wait_recv()
            through = jnp.exp(-slab_in[d - 1])
            for c in range(lines * cells):
                weight[c] *= jnp.broadcast_to(through[:, c : c + 1], tile)

    for l in range(lines):
        partial = weight[l * cells] * conc[emitter[l], 0]
        for b in range(1, cells):
            partial += weight[l * cells + b] * conc[emitter[l], b]
        sent[l + 1] = partial

    def out_copy(n):
        return pltpu.make_async_remote_copy(
            src_ref=sent,
            dst_ref=taken.at[n],
            send_sem=out_send,
            recv_sem=out_recv.at[n],
            device_id={"beam": 0},
            device_id_type=MESH,
        )

    def passed_copy(n):
        return pltpu.make_async_remote_copy(
            src_ref=passed_out.at[n],
            dst_ref=passed_in,
            send_sem=passed_send.at[n],
            recv_sem=passed_recv,
            device_id={"beam": n},
            device_id_type=MESH,
        )

    def ratio_copy(n):
        return pltpu.make_async_remote_copy(
            src_ref=ratios,
            dst_ref=ratios,
            send_sem=ratio_send.at[n],
            recv_sem=ratio_recv,
            device_id={"beam": n},
            device_id_type=MESH,
        )

    @pl.when(me > 0)
    def _():
        out_copy(me).start()

    @pl.when(me == 0)
    def _():
        loads[-1].wait()

        def one(n, carry):
            run, emission = carry
            passed = jnp.exp(-run)
            passed_out[n] = passed
            passed_copy(n).start()
            out_copy(n).wait_recv()
            emission = tuple(
                emission[l] + passed * taken[n, l + 1] for l in range(lines)
            )
            return run + taken[n, 0], emission

        first_part = tuple(sent[l + 1] for l in range(lines))
        _, emission = over(1, bricks, one, (sent[0], first_part))
        for l in range(lines):
            ratios[l] = data[tilt[0], l] / emission[l]

        def reply(n, carry):
            ratio_copy(n).start()
            return carry

        over(1, bricks, reply)
        passed_in[...] = jnp.ones(tile, jnp.float32)

    same = [
        [jnp.where(emitter[l] == emitter[k], 1.0, 0.0).astype(jnp.float32) for k in range(lines)]
        for l in range(lines)
    ]
    hit = [[emitter[l] == e for e in range(elements)] for l in range(lines)]

    @pl.when(me > 0)
    def _():
        passed_copy(me).wait_recv()
        ratio_copy(me).wait_recv()

    arrived = passed_in[...]
    ratio = [ratios[l] for l in range(lines)]
    for b in range(cells):
        kept = [weight[l * cells + b] * arrived for l in range(lines)]
        raised = [kept[l] * ratio[l] for l in range(lines)]
        factor = []
        for l in range(lines):
            top = blend_weight + raised[l]
            bottom = blend_weight + kept[l]
            for k in range(lines):
                if k != l:
                    top += same[l][k] * raised[k]
                    bottom += same[l][k] * kept[k]
            factor.append(top / bottom)
        for e in range(elements):
            scale = 1.0
            for l in range(lines):
                scale = jnp.where(hit[l][e], factor[l], scale)
            updated[e, b] = conc[e, b] * scale

    @pl.when(me > 0)
    def _():
        out_copy(me).wait_send()

    @pl.when(me == 0)
    def _():
        def done(n, carry):
            passed_copy(n).wait_send()
            ratio_copy(n).wait_send()
            return carry

        over(1, bricks, done)

    for d in range(1, slabs):
        pl.when(slab >= d)(lambda d=d: slab_copy(d, slab - d).wait_send())


def per_device(
    bricks, slabs, concentration, incident_mu, exit_mu, line_element, tilt_index, shear, data
):
    elements, cells, slices, width = concentration.shape
    lines = exit_mu.shape[0]
    f32 = jnp.float32
    arguments = (concentration, incident_mu, exit_mu, line_element, tilt_index, shear, data)
    return pl.pallas_call(
        functools.partial(kernel, bricks, slabs),
        out_shape=pltpu.VMEM(concentration.shape, f32),
        in_specs=[pl.BlockSpec(memory_space=pl.ANY)] * 7,
        out_specs=pl.BlockSpec(memory_space=pltpu.VMEM),
        scratch_shapes=[
            pltpu.VMEM(concentration.shape, f32),
            pltpu.VMEM(data.shape, f32),
            pltpu.SMEM(incident_mu.shape, f32),
            pltpu.SMEM(exit_mu.shape, f32),
            pltpu.SMEM(line_element.shape, jnp.int32),
            pltpu.SMEM(tilt_index.shape, jnp.int32),
            pltpu.SMEM(shear.shape, jnp.int32),
            pltpu.VMEM((2 * width, 2 * width), jnp.bfloat16),
            pltpu.VMEM((lines * cells, slices, width), f32),
            pltpu.VMEM((slices, width), f32),
            pltpu.VMEM((max(slabs - 1, 1), slices, width), f32),
            pltpu.VMEM((lines + 1, slices, width), f32),
            pltpu.VMEM((bricks, lines + 1, slices, width), f32),
            pltpu.VMEM((bricks, slices, width), f32),
            pltpu.VMEM((slices, width), f32),
            pltpu.VMEM((lines, slices, width), f32),
            pltpu.SemaphoreType.DMA((7,)),
            pltpu.SemaphoreType.DMA((max(slabs - 1, 1),)),
            pltpu.SemaphoreType.DMA((max(slabs - 1, 1),)),
            pltpu.SemaphoreType.DMA,
            pltpu.SemaphoreType.DMA((bricks,)),
            pltpu.SemaphoreType.DMA((bricks,)),
            pltpu.SemaphoreType.DMA,
            pltpu.SemaphoreType.DMA((bricks,)),
            pltpu.SemaphoreType.DMA,
        ],
        compiler_params=pltpu.CompilerParams(
            collective_id=0, has_side_effects=True, vmem_limit_bytes=16 * 1024 * 1024
        ),
        name="update",
    )(*(x if x.size == 1 else pltpu.with_memory_space_constraint(x, pltpu.HBM) for x in arguments))


def solution(mesh):
    placed = (
        P("grp", "beam", None, "gy"),
        P(),
        P(),
        P(),
        P(),
        P("grp"),
        P("grp", None, None, "gy"),
    )
    return jax.shard_map(
        functools.partial(per_device, mesh.shape["beam"], mesh.shape["gy"]),
        mesh=mesh,
        in_specs=placed,
        out_specs=P("grp", "beam", None, "gy"),
        check_vma=False,
    )
```

```python
import functools

import jax
import jax.numpy as jnp
from jax import lax
from jax.experimental import pallas as pl
from jax.experimental.pallas import tpu as pltpu
from jax.sharding import PartitionSpec as P

blend_weight = 0.05
MESH = pl.DeviceIdType.MESH


def over(start, stop, body, carry=0):
    if stop - start <= 16:
        for step in range(start, stop):
            carry = body(step, carry)
        return carry
    return lax.fori_loop(start, stop, body, carry)


def kernel(
    bricks,
    slabs,
    conc_hbm,
    incident_hbm,
    exit_hbm,
    line_hbm,
    tilt_hbm,
    shear_hbm,
    data_hbm,
    updated,
    conc,
    data,
    incident_mu,
    exit_mu,
    line,
    tilt,
    shear,
    sums,
    weight,
    light,
    through,
    total_out,
    total_in,
    slab_out,
    slab_in,
    sent,
    taken,
    passed_out,
    passed_in,
    ratios,
    load_sem,
    slab_send,
    slab_recv,
    total_send,
    total_recv,
    out_send,
    out_recv,
    passed_send,
    passed_recv,
    ratio_send,
    ratio_recv,
):
    elements, cells, slices, width = conc.shape
    lines = exit_mu.shape[0]
    me = lax.axis_index("beam")
    slab = lax.axis_index("gy")

    loads = [
        pltpu.make_async_copy(src, dst, load_sem.at[k])
        for k, (src, dst) in enumerate(
            (
                (conc_hbm, conc),
                (exit_hbm, exit_mu),
                (shear_hbm, shear),
                (incident_hbm, incident_mu),
                (line_hbm, line),
                (tilt_hbm, tilt),
                (data_hbm, data),
            )
        )
    ]
    for load in loads[:-1]:
        load.start()

    barrier = pltpu.get_barrier_semaphore()

    def greet(brick, place):
        pl.semaphore_signal(
            barrier, inc=1, device_id={"beam": brick, "gy": place}, device_id_type=MESH
        )

    for d in range(1, slabs):
        pl.when(slab + d < slabs)(lambda d=d: greet(me, slab + d))

    @pl.when(me == 0)
    def _():
        def one(n, carry):
            greet(n, slab)
            return carry

        over(1, bricks, one)
        loads[-1].start()

    pl.when(me > 0)(lambda: greet(0, slab))

    def side(shape, axis):
        return lax.broadcasted_iota(jnp.int32, shape, axis)

    square = (2 * width, 2 * width)
    row = lax.rem(side(square, 0), width)
    column = side(square, 1)
    sums[...] = jnp.where(
        column >= width, 1.0, jnp.where(row > column, 1.0, jnp.where(row == column, 0.5, 0.0))
    ).astype(jnp.bfloat16)

    tile = (slices, width)
    z_of = side(tile, 0)
    lane = side(tile, 1)
    for load in loads[1:-1]:
        load.wait()
    mu = [[exit_mu[l, e] for e in range(elements)] for l in range(lines)]
    mu_in = [incident_mu[e] for e in range(elements)]
    emitter = [line[l] for l in range(lines)]
    first = jnp.zeros(tile, jnp.int32)
    for z in range(slices):
        first = jnp.where(z_of == z, shear[z], first)
    support = [
        jnp.where(me * cells + b >= first, 1.0, 0.0).astype(jnp.float32) for b in range(cells)
    ]
    loads[0].wait()
    exit_rate = []
    for l in range(lines):
        for b in range(cells):
            total = conc[0, b] * mu[l][0]
            for e in range(1, elements):
                total += conc[e, b] * mu[l][e]
            exit_rate.append(total * support[b])
    stacked = jnp.concatenate(exit_rate, axis=0)
    high = stacked.astype(jnp.bfloat16)
    low = (stacked - high.astype(jnp.float32)).astype(jnp.bfloat16)
    terms = jnp.concatenate([high, low], axis=1)
    whole = jnp.dot(terms, sums[:, width:], preferred_element_type=jnp.float32)

    packed = jnp.zeros(tile, jnp.float32)
    for c in range(lines * cells):
        packed = jnp.where(lane == c, whole[c * slices : (c + 1) * slices], packed)
    slab_out[...] = packed

    def slab_copy(d, target):
        return pltpu.make_async_remote_copy(
            src_ref=slab_out,
            dst_ref=slab_in.at[d - 1],
            send_sem=slab_send.at[d - 1],
            recv_sem=slab_recv.at[d - 1],
            device_id={"gy": target},
            device_id_type=MESH,
        )

    pl.when(me == 0)(lambda: pl.semaphore_wait(barrier, bricks - 1 + slab))
    pl.when(me > 0)(lambda: pl.semaphore_wait(barrier, 1 + slab))
    for d in range(1, slabs):
        pl.when(slab >= d)(lambda d=d: slab_copy(d, slab - d).start())

    paths = jnp.dot(terms, sums[:, :width], preferred_element_type=jnp.float32)
    before = jnp.zeros(tile, jnp.float32)
    depth = []
    for b in range(cells):
        rate = conc[0, b] * mu_in[0]
        for e in range(1, elements):
            rate += conc[e, b] * mu_in[e]
        rate *= support[b]
        depth.append(before + 0.5 * rate)
        before += rate
    total_out[...] = before

    def total_copy(n):
        return pltpu.make_async_remote_copy(
            src_ref=total_out,
            dst_ref=total_in.at[n],
            send_sem=total_send,
            recv_sem=total_recv.at[n],
            device_id={"beam": 0},
            device_id_type=MESH,
        )

    def out_copy(n):
        return pltpu.make_async_remote_copy(
            src_ref=sent,
            dst_ref=taken.at[n],
            send_sem=out_send,
            recv_sem=out_recv.at[n],
            device_id={"beam": 0},
            device_id_type=MESH,
        )

    pl.when(me > 0)(lambda: total_copy(me).start())

    for l in range(lines):
        for b in range(cells):
            c = l * cells + b
            path = paths[c * slices : (c + 1) * slices]
            weight[c] = support[b] * jnp.exp(-(depth[b] + path))
            light[c] = weight[c] * conc[emitter[l], b]

    for d in range(1, slabs):

        @pl.when(slab + d < slabs)
        def _(d=d):
            slab_copy(d, slab).wait_recv()
            through[d - 1] = jnp.exp(-slab_in[d - 1])
            for c in range(lines * cells):
                light[c] *= jnp.broadcast_to(through[d - 1][:, c : c + 1], tile)

    for l in range(lines):
        partial = light[l * cells]
        for b in range(1, cells):
            partial += light[l * cells + b]
        sent[l] = partial

    def passed_copy(n):
        return pltpu.make_async_remote_copy(
            src_ref=passed_out.at[n],
            dst_ref=passed_in,
            send_sem=passed_send.at[n],
            recv_sem=passed_recv,
            device_id={"beam": n},
            device_id_type=MESH,
        )

    def ratio_copy(n):
        return pltpu.make_async_remote_copy(
            src_ref=ratios,
            dst_ref=ratios,
            send_sem=ratio_send.at[n],
            recv_sem=ratio_recv,
            device_id={"beam": n},
            device_id_type=MESH,
        )

    pl.when(me > 0)(lambda: out_copy(me).start())

    same = [
        [jnp.where(emitter[l] == emitter[k], 1.0, 0.0).astype(jnp.float32) for k in range(lines)]
        for l in range(lines)
    ]
    hit = [[emitter[l] == e for e in range(elements)] for l in range(lines)]

    for d in range(1, slabs):

        @pl.when(slab + d < slabs)
        def _(d=d):
            for c in range(lines * cells):
                weight[c] *= jnp.broadcast_to(through[d - 1][:, c : c + 1], tile)

    def prepare():
        arrived = passed_in[...]
        for b in range(cells):
            kept = [weight[l * cells + b] * arrived for l in range(lines)]
            for l in range(lines):
                bottom = blend_weight + kept[l]
                for k in range(lines):
                    if k != l:
                        bottom += same[l][k] * kept[k]
                weight[l * cells + b] = kept[l]
                light[l * cells + b] = 1.0 / bottom

    @pl.when(me == 0)
    def _():
        passed_in[...] = jnp.ones(tile, jnp.float32)

    pl.when(me > 0)(lambda: passed_copy(me).wait_recv())
    prepare()

    @pl.when(me == 0)
    def _():
        loads[-1].wait()

        def ahead(n, run):
            passed_out[n] = jnp.exp(-run)
            passed_copy(n).start()
            total_copy(n).wait_recv()
            return run + total_in[n]

        over(1, bricks, ahead, total_out[...])

        def one(n, emission):
            out_copy(n).wait_recv()
            return tuple(emission[l] + passed_out[n] * taken[n, l] for l in range(lines))

        emission = over(1, bricks, one, tuple(sent[l] for l in range(lines)))
        for l in range(lines):
            ratios[l] = data[tilt[0], l] / emission[l]

        def reply(n, carry):
            ratio_copy(bricks - n).start()
            return carry

        over(1, bricks, reply)

    pl.when(me > 0)(lambda: ratio_copy(me).wait_recv())
    ratio = [ratios[l] for l in range(lines)]
    for b in range(cells):
        raised = [weight[l * cells + b] * ratio[l] for l in range(lines)]
        factor = []
        for l in range(lines):
            top = blend_weight + raised[l]
            for k in range(lines):
                if k != l:
                    top += same[l][k] * raised[k]
            factor.append(top * light[l * cells + b])
        for e in range(elements):
            scale = 1.0
            for l in range(lines):
                scale = jnp.where(hit[l][e], factor[l], scale)
            updated[e, b] = conc[e, b] * scale

    @pl.when(me > 0)
    def _():
        total_copy(me).wait_send()
        out_copy(me).wait_send()

    @pl.when(me == 0)
    def _():
        def done(n, carry):
            passed_copy(n).wait_send()
            ratio_copy(n).wait_send()
            return carry

        over(1, bricks, done)

    for d in range(1, slabs):
        pl.when(slab >= d)(lambda d=d: slab_copy(d, slab - d).wait_send())


def per_device(
    bricks, slabs, concentration, incident_mu, exit_mu, line_element, tilt_index, shear, data
):
    elements, cells, slices, width = concentration.shape
    lines = exit_mu.shape[0]
    f32 = jnp.float32
    arguments = (concentration, incident_mu, exit_mu, line_element, tilt_index, shear, data)
    return pl.pallas_call(
        functools.partial(kernel, bricks, slabs),
        out_shape=pltpu.VMEM(concentration.shape, f32),
        in_specs=[pl.BlockSpec(memory_space=pl.ANY)] * 7,
        out_specs=pl.BlockSpec(memory_space=pltpu.VMEM),
        scratch_shapes=[
            pltpu.VMEM(concentration.shape, f32),
            pltpu.VMEM(data.shape, f32),
            pltpu.SMEM(incident_mu.shape, f32),
            pltpu.SMEM(exit_mu.shape, f32),
            pltpu.SMEM(line_element.shape, jnp.int32),
            pltpu.SMEM(tilt_index.shape, jnp.int32),
            pltpu.SMEM(shear.shape, jnp.int32),
            pltpu.VMEM((2 * width, 2 * width), jnp.bfloat16),
            pltpu.VMEM((lines * cells, slices, width), f32),
            pltpu.VMEM((lines * cells, slices, width), f32),
            pltpu.VMEM((max(slabs - 1, 1), slices, width), f32),
            pltpu.VMEM((slices, width), f32),
            pltpu.VMEM((bricks, slices, width), f32),
            pltpu.VMEM((slices, width), f32),
            pltpu.VMEM((max(slabs - 1, 1), slices, width), f32),
            pltpu.VMEM((lines, slices, width), f32),
            pltpu.VMEM((bricks, lines, slices, width), f32),
            pltpu.VMEM((bricks, slices, width), f32),
            pltpu.VMEM((slices, width), f32),
            pltpu.VMEM((lines, slices, width), f32),
            pltpu.SemaphoreType.DMA((7,)),
            pltpu.SemaphoreType.DMA((max(slabs - 1, 1),)),
            pltpu.SemaphoreType.DMA((max(slabs - 1, 1),)),
            pltpu.SemaphoreType.DMA,
            pltpu.SemaphoreType.DMA((bricks,)),
            pltpu.SemaphoreType.DMA,
            pltpu.SemaphoreType.DMA((bricks,)),
            pltpu.SemaphoreType.DMA((bricks,)),
            pltpu.SemaphoreType.DMA,
            pltpu.SemaphoreType.DMA((bricks,)),
            pltpu.SemaphoreType.DMA,
        ],
        compiler_params=pltpu.CompilerParams(
            collective_id=0, has_side_effects=True, vmem_limit_bytes=16 * 1024 * 1024
        ),
        name="update",
    )(*(x if x.size == 1 else pltpu.with_memory_space_constraint(x, pltpu.HBM) for x in arguments))


def solution(mesh):
    placed = (
        P("grp", "beam", None, "gy"),
        P(),
        P(),
        P(),
        P(),
        P("grp"),
        P("grp", None, None, "gy"),
    )
    return jax.shard_map(
        functools.partial(per_device, mesh.shape["beam"], mesh.shape["gy"]),
        mesh=mesh,
        in_specs=placed,
        out_specs=P("grp", "beam", None, "gy"),
        check_vma=False,
    )
```

```python
import functools

import jax
import jax.numpy as jnp
from jax import lax
from jax.experimental import pallas as pl
from jax.experimental.pallas import tpu as pltpu
from jax.sharding import PartitionSpec as P

blend_weight = 0.05
MESH = pl.DeviceIdType.MESH


def over(start, stop, body, carry=0):
    if stop - start <= 16:
        for step in range(start, stop):
            carry = body(step, carry)
        return carry
    return lax.fori_loop(start, stop, body, carry)


def kernel(
    bricks,
    slabs,
    conc_hbm,
    incident_hbm,
    exit_hbm,
    line_hbm,
    tilt_hbm,
    shear_hbm,
    data_hbm,
    updated,
    conc,
    data,
    incident_mu,
    exit_mu,
    line,
    tilt,
    shear,
    sums,
    weight,
    light,
    through,
    total_out,
    total_in,
    slab_out,
    slab_in,
    sent,
    taken,
    passed_out,
    passed_in,
    ratios,
    load_sem,
    slab_send,
    slab_recv,
    total_send,
    total_recv,
    out_send,
    out_recv,
    passed_send,
    passed_recv,
    ratio_send,
    ratio_recv,
):
    elements, cells, slices, width = conc.shape
    lines = exit_mu.shape[0]
    me = lax.axis_index("beam")
    slab = lax.axis_index("gy")

    loads = [
        pltpu.make_async_copy(src, dst, load_sem.at[k])
        for k, (src, dst) in enumerate(
            (
                (conc_hbm, conc),
                (exit_hbm, exit_mu),
                (shear_hbm, shear),
                (incident_hbm, incident_mu),
                (line_hbm, line),
                (tilt_hbm, tilt),
                (data_hbm, data),
            )
        )
    ]
    for load in loads[:-1]:
        load.start()

    barrier = pltpu.get_barrier_semaphore()

    def greet(brick, place):
        pl.semaphore_signal(
            barrier, inc=1, device_id={"beam": brick, "gy": place}, device_id_type=MESH
        )

    for d in range(1, slabs):
        pl.when(slab + d < slabs)(lambda d=d: greet(me, slab + d))

    @pl.when(me == 0)
    def _():
        def one(n, carry):
            greet(n, slab)
            return carry

        over(1, bricks, one)
        loads[-1].start()

    even = lax.rem(me, 2) == 0
    hands_on = jnp.logical_and(even, jnp.logical_and(me > 0, me + 1 < bricks))
    plain = jnp.logical_and(me > 0, jnp.logical_not(hands_on))
    pl.when(me > 0)(lambda: greet(0, slab))
    pl.when(jnp.logical_and(jnp.logical_not(even), me > 1))(lambda: greet(me - 1, slab))

    def side(shape, axis):
        return lax.broadcasted_iota(jnp.int32, shape, axis)

    square = (2 * width, 2 * width)
    row = lax.rem(side(square, 0), width)
    column = side(square, 1)
    sums[...] = jnp.where(
        column >= width, 1.0, jnp.where(row > column, 1.0, jnp.where(row == column, 0.5, 0.0))
    ).astype(jnp.bfloat16)

    tile = (slices, width)
    z_of = side(tile, 0)
    lane = side(tile, 1)
    for load in loads[1:-1]:
        load.wait()
    mu = [[exit_mu[l, e] for e in range(elements)] for l in range(lines)]
    mu_in = [incident_mu[e] for e in range(elements)]
    emitter = [line[l] for l in range(lines)]
    first = jnp.zeros(tile, jnp.int32)
    for z in range(slices):
        first = jnp.where(z_of == z, shear[z], first)
    support = [
        jnp.where(me * cells + b >= first, 1.0, 0.0).astype(jnp.float32) for b in range(cells)
    ]
    loads[0].wait()
    exit_rate = []
    for l in range(lines):
        for b in range(cells):
            total = conc[0, b] * mu[l][0]
            for e in range(1, elements):
                total += conc[e, b] * mu[l][e]
            exit_rate.append(total * support[b])
    stacked = jnp.concatenate(exit_rate, axis=0)
    high = stacked.astype(jnp.bfloat16)
    low = (stacked - high.astype(jnp.float32)).astype(jnp.bfloat16)
    terms = jnp.concatenate([high, low], axis=1)
    whole = jnp.dot(terms, sums[:, width:], preferred_element_type=jnp.float32)

    packed = jnp.zeros(tile, jnp.float32)
    for c in range(lines * cells):
        packed = jnp.where(lane == c, whole[c * slices : (c + 1) * slices], packed)
    slab_out[...] = packed

    def slab_copy(d, target):
        return pltpu.make_async_remote_copy(
            src_ref=slab_out,
            dst_ref=slab_in.at[d - 1],
            send_sem=slab_send.at[d - 1],
            recv_sem=slab_recv.at[d - 1],
            device_id={"gy": target},
            device_id_type=MESH,
        )

    pl.when(me == 0)(lambda: pl.semaphore_wait(barrier, bricks - 1 + slab))
    pl.when(hands_on)(lambda: pl.semaphore_wait(barrier, 2 + slab))
    pl.when(plain)(lambda: pl.semaphore_wait(barrier, 1 + slab))
    for d in range(1, slabs):
        pl.when(slab >= d)(lambda d=d: slab_copy(d, slab - d).start())

    paths = jnp.dot(terms, sums[:, :width], preferred_element_type=jnp.float32)
    before = jnp.zeros(tile, jnp.float32)
    depth = []
    for b in range(cells):
        rate = conc[0, b] * mu_in[0]
        for e in range(1, elements):
            rate += conc[e, b] * mu_in[e]
        rate *= support[b]
        depth.append(before + 0.5 * rate)
        before += rate
    total_out[...] = before

    def total_copy(n):
        return pltpu.make_async_remote_copy(
            src_ref=total_out,
            dst_ref=total_in.at[n],
            send_sem=total_send,
            recv_sem=total_recv.at[n],
            device_id={"beam": 0},
            device_id_type=MESH,
        )

    def out_copy(n):
        return pltpu.make_async_remote_copy(
            src_ref=sent,
            dst_ref=taken.at[n],
            send_sem=out_send,
            recv_sem=out_recv.at[n],
            device_id={"beam": 0},
            device_id_type=MESH,
        )

    pl.when(me > 0)(lambda: total_copy(me).start())

    for l in range(lines):
        for b in range(cells):
            c = l * cells + b
            path = paths[c * slices : (c + 1) * slices]
            weight[c] = support[b] * jnp.exp(-(depth[b] + path))
            light[c] = weight[c] * conc[emitter[l], b]

    for d in range(1, slabs):

        @pl.when(slab + d < slabs)
        def _(d=d):
            slab_copy(d, slab).wait_recv()
            through[d - 1] = jnp.exp(-slab_in[d - 1])
            for c in range(lines * cells):
                light[c] *= jnp.broadcast_to(through[d - 1][:, c : c + 1], tile)

    for l in range(lines):
        partial = light[l * cells]
        for b in range(1, cells):
            partial += light[l * cells + b]
        sent[l] = partial

    def passed_copy(n):
        return pltpu.make_async_remote_copy(
            src_ref=passed_out.at[n],
            dst_ref=passed_in,
            send_sem=passed_send.at[n],
            recv_sem=passed_recv,
            device_id={"beam": n},
            device_id_type=MESH,
        )

    def ratio_copy(n):
        return pltpu.make_async_remote_copy(
            src_ref=ratios,
            dst_ref=ratios,
            send_sem=ratio_send.at[n],
            recv_sem=ratio_recv,
            device_id={"beam": n},
            device_id_type=MESH,
        )

    pl.when(me > 0)(lambda: out_copy(me).start())

    same = [
        [jnp.where(emitter[l] == emitter[k], 1.0, 0.0).astype(jnp.float32) for k in range(lines)]
        for l in range(lines)
    ]
    hit = [[emitter[l] == e for e in range(elements)] for l in range(lines)]

    for d in range(1, slabs):

        @pl.when(slab + d < slabs)
        def _(d=d):
            for c in range(lines * cells):
                weight[c] *= jnp.broadcast_to(through[d - 1][:, c : c + 1], tile)

    def prepare():
        arrived = passed_in[...]
        for b in range(cells):
            kept = [weight[l * cells + b] * arrived for l in range(lines)]
            for l in range(lines):
                bottom = blend_weight + kept[l]
                for k in range(lines):
                    if k != l:
                        bottom += same[l][k] * kept[k]
                weight[l * cells + b] = kept[l]
                light[l * cells + b] = 1.0 / bottom

    @pl.when(me == 0)
    def _():
        passed_in[...] = jnp.ones(tile, jnp.float32)

    pl.when(me > 0)(lambda: passed_copy(me).wait_recv())
    prepare()

    @pl.when(me == 0)
    def _():
        loads[-1].wait()

        def ahead(n, run):
            passed_out[n] = jnp.exp(-run)
            passed_copy(n).start()
            total_copy(n).wait_recv()
            return run + total_in[n]

        over(1, bricks, ahead, total_out[...])

        def one(n, emission):
            out_copy(n).wait_recv()
            return tuple(emission[l] + passed_out[n] * taken[n, l] for l in range(lines))

        emission = over(1, bricks, one, tuple(sent[l] for l in range(lines)))
        for l in range(lines):
            ratios[l] = data[tilt[0], l] / emission[l]

        def reply(k, carry):
            ratio_copy(2 * k).start()
            return carry

        over(1, (bricks + 1) // 2, reply)
        if bricks > 1:
            ratio_copy(1).start()

    pl.when(me > 0)(lambda: ratio_copy(me).wait_recv())
    pl.when(hands_on)(lambda: ratio_copy(me + 1).start())
    ratio = [ratios[l] for l in range(lines)]
    for b in range(cells):
        raised = [weight[l * cells + b] * ratio[l] for l in range(lines)]
        factor = []
        for l in range(lines):
            top = blend_weight + raised[l]
            for k in range(lines):
                if k != l:
                    top += same[l][k] * raised[k]
            factor.append(top * light[l * cells + b])
        for e in range(elements):
            scale = 1.0
            for l in range(lines):
                scale = jnp.where(hit[l][e], factor[l], scale)
            updated[e, b] = conc[e, b] * scale

    @pl.when(me > 0)
    def _():
        total_copy(me).wait_send()
        out_copy(me).wait_send()

    @pl.when(me == 0)
    def _():
        def done(n, carry):
            passed_copy(n).wait_send()
            return carry

        over(1, bricks, done)

        def replied(k, carry):
            ratio_copy(2 * k).wait_send()
            return carry

        over(1, (bricks + 1) // 2, replied)
        if bricks > 1:
            ratio_copy(1).wait_send()

    pl.when(hands_on)(lambda: ratio_copy(me + 1).wait_send())

    for d in range(1, slabs):
        pl.when(slab >= d)(lambda d=d: slab_copy(d, slab - d).wait_send())


def per_device(
    bricks, slabs, concentration, incident_mu, exit_mu, line_element, tilt_index, shear, data
):
    elements, cells, slices, width = concentration.shape
    lines = exit_mu.shape[0]
    f32 = jnp.float32
    arguments = (concentration, incident_mu, exit_mu, line_element, tilt_index, shear, data)
    return pl.pallas_call(
        functools.partial(kernel, bricks, slabs),
        out_shape=pltpu.VMEM(concentration.shape, f32),
        in_specs=[pl.BlockSpec(memory_space=pl.ANY)] * 7,
        out_specs=pl.BlockSpec(memory_space=pltpu.VMEM),
        scratch_shapes=[
            pltpu.VMEM(concentration.shape, f32),
            pltpu.VMEM(data.shape, f32),
            pltpu.SMEM(incident_mu.shape, f32),
            pltpu.SMEM(exit_mu.shape, f32),
            pltpu.SMEM(line_element.shape, jnp.int32),
            pltpu.SMEM(tilt_index.shape, jnp.int32),
            pltpu.SMEM(shear.shape, jnp.int32),
            pltpu.VMEM((2 * width, 2 * width), jnp.bfloat16),
            pltpu.VMEM((lines * cells, slices, width), f32),
            pltpu.VMEM((lines * cells, slices, width), f32),
            pltpu.VMEM((max(slabs - 1, 1), slices, width), f32),
            pltpu.VMEM((slices, width), f32),
            pltpu.VMEM((bricks, slices, width), f32),
            pltpu.VMEM((slices, width), f32),
            pltpu.VMEM((max(slabs - 1, 1), slices, width), f32),
            pltpu.VMEM((lines, slices, width), f32),
            pltpu.VMEM((bricks, lines, slices, width), f32),
            pltpu.VMEM((bricks, slices, width), f32),
            pltpu.VMEM((slices, width), f32),
            pltpu.VMEM((lines, slices, width), f32),
            pltpu.SemaphoreType.DMA((7,)),
            pltpu.SemaphoreType.DMA((max(slabs - 1, 1),)),
            pltpu.SemaphoreType.DMA((max(slabs - 1, 1),)),
            pltpu.SemaphoreType.DMA,
            pltpu.SemaphoreType.DMA((bricks,)),
            pltpu.SemaphoreType.DMA,
            pltpu.SemaphoreType.DMA((bricks,)),
            pltpu.SemaphoreType.DMA((bricks,)),
            pltpu.SemaphoreType.DMA,
            pltpu.SemaphoreType.DMA((bricks,)),
            pltpu.SemaphoreType.DMA,
        ],
        compiler_params=pltpu.CompilerParams(
            collective_id=0, has_side_effects=True, vmem_limit_bytes=16 * 1024 * 1024
        ),
        name="update",
    )(*(x if x.size == 1 else pltpu.with_memory_space_constraint(x, pltpu.HBM) for x in arguments))


def solution(mesh):
    placed = (
        P("grp", "beam", None, "gy"),
        P(),
        P(),
        P(),
        P(),
        P("grp"),
        P("grp", None, None, "gy"),
    )
    return jax.shard_map(
        functools.partial(per_device, mesh.shape["beam"], mesh.shape["gy"]),
        mesh=mesh,
        in_specs=placed,
        out_specs=P("grp", "beam", None, "gy"),
        check_vma=False,
    )
```
